256 devices in a mesh: seq: 32 (over y, z), head: 8 (over x, core).
Axes of the slice: x: 4, y: 4, z: 8, core: 2. Of those that a mesh axis runs over, the one named last changes fastest.
Arguments:
- query_act: bfloat16 [32768, 8192], P('seq', 'head'), may hold values from -6 to 6
- key_act: bfloat16 [32768, 8192], P('seq', 'head'), may hold values from -6 to 6
- value_act: bfloat16 [32768, 8192], P('seq', 'head'), may hold values from -170 to 170
- norm_gain: bfloat16 [8192], P('head'), may hold values from 0.099609375 to 1.8984375
- doc_lengths: int32 [64], replicated, may hold values from 1 to 8192, 32768 in all
Outputs:
- attended: bfloat16 [32768, 8192], P('seq', 'head')
The draws below stay inside these ranges and needn't reach their ends.
All inputs are finite; a program needn't handle non-finite values.
Results may differ from the reference program's by a relative error of at most 0.0043.
Values sent between devices are 32-bit elements; how exact they have to be, the bound alone decides.
A program may use at most 128 MiB of HBM per device.

```python
import math
import jax
import jax.numpy as jnp
import numpy as np
from jax import lax

HEADS = 64
E = 128
TOK_DEV = 1024
TOKENS = 32768
DOCS = 64
N_SEQ = 32


def draw_value_act(key, part):
    key = jax.random.fold_in(key, 11)
    base_key = jax.random.fold_in(key, 0)
    head_pos = jnp.arange(HEADS * E, dtype=jnp.int32) // E
    column_scale = 10.0 ** (head_pos.astype(jnp.float32) / max(HEADS - 1, 1))
    samples = jax.random.normal(base_key, (TOKENS, HEADS * E), jnp.float32)
    return (jnp.clip(samples, -5.0, 5.0) * column_scale[None, :]).astype(jnp.bfloat16)


def shard_levels(rng, dims, cuts, low, high):
    loudness = 1.0
    for axis_at, shards_of in cuts:
        heights = jax.random.uniform(jax.random.fold_in(jax.random.fold_in(rng, 6), axis_at), (shards_of,), jnp.float32, low / len(cuts), high / len(cuts))
        loudness = loudness * jnp.repeat(jnp.exp(heights), dims[axis_at] // shards_of).reshape((-1,) + (1,) * (len(dims) - 1 - axis_at))
    return loudness


def profile(amount, total, bound, slope):
    weights = [(1 << 20) // math.isqrt(rank ** slope) + 1 for rank in range(2, amount + 1)]
    spare, holding = total - bound - (amount - 1), [1] * (amount - 1)
    while spare > 0:
        free = [i for i in range(amount - 1) if holding[i] < bound]
        whole, budget = sum([weights[i] for i in free]), spare
        for i in free:
            more = min(bound - holding[i], max(1, budget * weights[i] // whole), spare)
            holding[i] = holding[i] + more
            spare = spare - more
    return np.array([bound] + holding)


def uneven(own_key, amount, total, limit, slope):
    if amount == 2:
        one = jax.random.randint(own_key, (), max(1, total - limit), min(limit, total - 1) + 1)
        return jnp.stack([one, total - one])
    tallies = jnp.asarray(profile(amount, total, limit, slope), jnp.int32)
    couples = (amount - 1) // 2
    giver, taker = tallies[1:1 + 2 * couples:2], tallies[2:2 + 2 * couples:2]
    slack = jnp.minimum(giver - 1, limit - taker)
    moved = jax.random.randint(jax.random.fold_in(own_key, 1), (couples,), 0, 1 << 20) % (slack + 1)
    tallies = tallies.at[1:1 + 2 * couples:2].set(giver - moved).at[2:2 + 2 * couples:2].set(taker + moved)
    return tallies[jax.random.permutation(jax.random.fold_in(own_key, 2), amount)]


def centred(own_key, shape, spread, most, shards=(), kind=jnp.bfloat16):
    values = spread * jax.random.normal(own_key, shape, jnp.float32)
    if shards:
        values = values * shard_levels(own_key, shape, shards, -0.22, 0.18)
    return jnp.clip(values, -most, most).astype(kind)


def setup_inputs(seed: int = 0) -> dict:
    keys = jax.random.split(jax.random.key(seed), 6)
    query_act = centred(keys[0], (TOKENS, HEADS * E), 1.0, 6.0, ((0, 32), (1, 8)))
    key_act = centred(keys[1], (TOKENS, HEADS * E), 1.0, 6.0, ((0, 32), (1, 8)))
    value_act = draw_value_act(jax.random.fold_in(keys[5], 71), 0)
    norm_gain = jnp.clip(1.0 + 0.18 * jax.random.normal(keys[3], (HEADS * E,), jnp.float32), 0.099609375, 1.8984375).astype(jnp.bfloat16)
    doc_lengths = uneven(keys[4], DOCS, TOKENS, TOKENS // 4, 2).astype(jnp.int32)
    return {"query_act": query_act, "key_act": key_act, "value_act": value_act, "norm_gain": norm_gain, "doc_lengths": doc_lengths}


def feature_map(inputs):
    return (jax.nn.elu(inputs.astype(jnp.float32)) + 1.0).astype(jnp.bfloat16)

def doc_index(positions, doc_lengths):
    doc_ends = jnp.cumsum(doc_lengths, dtype=jnp.int32)
    return lax.optimization_barrier(jnp.sum((doc_ends[None, :] <= positions[:, None]).astype(jnp.int32), axis=1, dtype=jnp.int32))

def reference(query_act, key_act, value_act, norm_gain, doc_lengths):
    feat_width = HEADS * E
    query_shards = query_act.reshape(N_SEQ, TOK_DEV, HEADS, E)
    key_shards = key_act.reshape(N_SEQ, TOK_DEV, HEADS, E)
    value_shards = value_act.reshape(N_SEQ, TOK_DEV, HEADS, E)
    gain_wide = norm_gain.astype(jnp.float32)
    offsets = jnp.arange(TOK_DEV, dtype=jnp.int32)
    causal = offsets[:, None] >= offsets[None, :]

    def shard_step(pending, inputs_now):
        waiting_state, pending_norm = pending
        shard_id, query_rows, key_rows, value_rows = inputs_now
        positions = shard_id * TOK_DEV + offsets
        doc_ids = doc_index(positions, doc_lengths)
        prev_last = doc_index(jnp.reshape(shard_id * TOK_DEV - 1, (1,)).astype(jnp.int32), doc_lengths)[0]
        follow = ((doc_ids[0] == prev_last) & (shard_id > 0)).astype(jnp.float32)
        starts = (doc_ids[TOK_DEV - 1] != prev_last).astype(jnp.float32)
        query_feats = lax.optimization_barrier(feature_map(query_rows)).astype(jnp.float32)
        key_feats = lax.optimization_barrier(feature_map(key_rows)).astype(jnp.float32)
        value_full_width = value_rows.astype(jnp.float32)
        scores = jnp.einsum('qhe,khe->hqk', query_feats, key_feats)
        retain = causal & (doc_ids[:, None] == doc_ids[None, :])
        masked_scores = jnp.where(retain[None], scores, 0.0)
        local_den = lax.optimization_barrier(jnp.sum(masked_scores, axis=2)).T
        weights = lax.optimization_barrier(masked_scores.astype(jnp.bfloat16)).astype(jnp.float32)
        local_num = jnp.einsum('hqk,khe->qhe', weights, value_full_width)
        carried_state = follow * waiting_state
        carried_norm = follow * pending_norm
        carry_num = jnp.einsum('qhe,hef->qhf', query_feats, carried_state, precision=lax.Precision.HIGHEST)
        carry_den = jnp.einsum('qhe,he->qh', query_feats, carried_norm, precision=lax.Precision.HIGHEST)
        inside_first_document = doc_ids == doc_ids[0]
        numerator = local_num + jnp.where(inside_first_document[:, None, None], carry_num, 0.0)
        denominator = local_den + jnp.where(inside_first_document[:, None], carry_den, 0.0)
        attention = numerator / denominator[:, :, None]
        flattened = attention.reshape(TOK_DEV, feat_width)
        mean_square = lax.optimization_barrier(jnp.mean(flattened * flattened, axis=1, keepdims=True))
        attended = (flattened * lax.rsqrt(mean_square + 1e-06) * gain_wide).astype(jnp.bfloat16)
        trailing_keys = jnp.where((doc_ids == doc_ids[TOK_DEV - 1])[:, None, None], key_feats, 0.0)
        trailing_state = jnp.einsum('uzb,uzi->zbi', trailing_keys, value_full_width)
        tail_norm = lax.optimization_barrier(jnp.sum(trailing_keys, axis=0))
        keep_old = 1.0 - starts
        return ((trailing_state + keep_old * waiting_state, tail_norm + keep_old * pending_norm), attended)
    initial = (jnp.zeros((HEADS, E, E), jnp.float32), jnp.zeros((HEADS, E), jnp.float32))
    shard_ids = jnp.arange(N_SEQ, dtype=jnp.int32)
    final_carry, outputs = lax.scan(shard_step, initial, (shard_ids, query_shards, key_shards, value_shards))
    return outputs.reshape(TOKENS, feat_width)
```

```python
import functools

import jax
import jax.numpy as jnp
from jax import lax
from jax.experimental import pallas as pl
from jax.experimental.pallas import tpu as pltpu
from jax.sharding import PartitionSpec as P

E = 128
ROWS = 136
MESH = pl.DeviceIdType.MESH
F32 = jnp.float32
BF16 = jnp.bfloat16
H1_SLOT, H2_SLOT, H3_SLOT = 0, 3, 6


def feature_map(x):
    x = x.astype(F32)
    return jnp.where(x > 0.0, x + 1.0, jnp.exp(x)).astype(BF16)


def kernel(
    n_seq, n_head, n_feat,
    q_hbm, k_hbm, v_hbm, len_ref,
    att_hbm, scale_ref,
    qraw, kraw, vraw, qf, kft, tails, nd, att, sqacc,
    mask, cmask, tmask, dl, df,
    wr, sr, yr, tr, wo, so, tm, sq,
    in_sem, out_sem,
    wr_s, wr_r, sr_s, sr_r, yr_s, yr_r, tr_s, tr_r, sq_s, sq_r,
):
    heads, tok, _ = qraw.shape
    groups = tok // 128
    i = lax.axis_index("seq")
    hd = lax.axis_index("head")

    def shard(d):
        return (lax.rem(i + d + n_seq, n_seq), hd)

    def peer(j):
        return (i, lax.rem(hd + j, n_head))

    def position(j):
        return jnp.where(j < 4, 3 * lax.rem(j, 2), 1 + lax.rem(j, 2))

    def head_of(p, u):
        return lax.rem(i - p + 4 * n_seq, 4) + 4 * u

    def col(ref, h):
        return ref.at[:, pl.ds(pl.multiple_of(h * E, E), E)]

    def load(which, h):
        src, dst = ((q_hbm, qraw), (k_hbm, kraw), (v_hbm, vraw))[which]
        return pltpu.make_async_copy(col(src, h), dst.at[h], in_sem.at[which, h])

    barrier = pltpu.get_barrier_semaphore()
    senders = [shard(d) for d in (-1, 1, -8, -3, -5, -7)]
    senders += [peer(j) for j in range(1, n_head)]
    for dev in senders:
        pl.semaphore_signal(barrier, inc=1, device_id=dev, device_id_type=MESH)

    @pl.loop(0, heads)
    def _(j):
        h = head_of(position(j), lax.rem(j // 2, 2))
        load(1, h).start()
        load(2, h).start()

    @pl.loop(0, heads)
    def _(h):
        load(0, h).start()

    base = i * tok
    lane8 = lax.broadcasted_iota(jnp.int32, (8, 128), 1)
    sub8 = lax.broadcasted_iota(jnp.int32, (8, 128), 0)
    sub16 = lax.broadcasted_iota(jnp.int32, (16, 128), 0)
    pos_tok = base + sub8 * 128 + lane8
    pos_last = (i - 7 + sub16) * tok - 1
    pos_first = jnp.zeros((8, 128), jnp.int32) + base
    st_tok = jnp.zeros((8, 128), jnp.int32)
    st_last = jnp.where(pos_last < 0, -1, 0)
    st_first = jnp.zeros((8, 128), jnp.int32)
    end = jnp.int32(0)
    for d in range(len_ref.shape[0]):
        end = end + len_ref[d]
        st_tok = jnp.where(pos_tok >= end, end, st_tok)
        st_last = jnp.where(pos_last >= end, end, st_last)
        st_first = jnp.where(pos_first >= end, end, st_first)
    dl[...] = st_last
    df[...] = st_first

    lane = lax.broadcasted_iota(jnp.int32, (128, 128), 1).astype(F32)
    sub = lax.broadcasted_iota(jnp.int32, (128, 128), 0).astype(F32)
    st_loc = (st_tok - base).astype(F32)
    tail_start = (st_last[8:9, :] - base).astype(F32)
    one, zero = jnp.ones((128, 128), F32), jnp.zeros((128, 128), F32)
    for g in range(groups):
        first = jnp.broadcast_to(st_loc[g : g + 1, :], (128, 128)).T
        rows = pl.ds(g * 128, 128)
        cmask[rows, :] = jnp.where(first <= 0.0, one, zero).astype(BF16)
        tmask[:, rows] = jnp.where(lane + 128.0 * g >= tail_start, one, zero).astype(BF16)
        for k in range(2 * (g // 2) + 2):
            s = lane + 128.0 * k
            keep = s >= first
            if k == g:
                keep = keep & (lane <= sub)
            value = jnp.where(keep, one, zero) if k <= g else zero
            mask[rows, pl.ds(k * 128, 128)] = value.astype(BF16)

    pl.semaphore_wait(barrier, len(senders))

    ones_v = jnp.ones((tok, 128), BF16)

    def send(src, dst, s_sem, r_sem, dev):
        return pltpu.make_async_remote_copy(
            src_ref=src, dst_ref=dst, send_sem=s_sem, recv_sem=r_sem, device_id=dev, device_id_type=MESH
        )

    def send_w(p, u, src):
        return send(src, wr.at[p - 1, u], wr_s.at[p - 1, u], wr_r.at[p - 1, u], shard(1))

    def send_s(p, u, src):
        return send(src, sr.at[p, u], sr_s.at[p, u], sr_r.at[p, u], shard(-1))

    def send_y(p, u, src):
        return send(src, yr.at[p, u], yr_s.at[p, u], yr_r.at[p, u], shard(8))

    def send_t(p, u, src):
        dist = (1, 3, 5, 7)[p]
        return send(src, tr.at[p, u], tr_s.at[p, u], tr_r.at[p, u], shard(dist))

    @pl.loop(0, heads)
    def _(j):
        p = position(j)
        u = lax.rem(j // 2, 2)
        h = head_of(p, u)
        load(1, h).wait()
        kt = feature_map(kraw[h]).T
        kft[h] = kt
        load(2, h).wait()
        state = jnp.dot(
            kt * tmask[...],
            jnp.concatenate([vraw[h], ones_v], axis=1),
            preferred_element_type=F32,
        )
        tails[h, pl.ds(0, 128), :] = state[:, :128]
        tails[h, pl.ds(128, 8), :] = state[:, 128:].T[0:8, :]

        @pl.when((j < 4) & (p == 0))
        def _():
            send_w(1, u, tails.at[h]).start()

        @pl.when((j < 4) & (p == 3))
        def _():
            send_s(2, u, tails.at[h]).start()
            send_y(3, u, tails.at[h]).start()

    def row(r):
        return dl[pl.ds(r, 1), :]

    def gated(cond, x):
        return jnp.where(cond, x, 0.0)

    keep = lambda: row(8) == row(7)

    def handle_1(u):
        send_w(1, u, wo.at[0, u]).wait_recv()
        wo[0, u] = tails[head_of(1, u)] + gated(keep(), wr[0, u])
        send_w(2, u, wo.at[0, u]).start()
        send_s(2, u, so.at[2, u]).wait_recv()
        so[2, u] = gated(row(8) == row(9), tails[head_of(2, u)]) + sr[2, u]
        send_s(1, u, so.at[2, u]).start()
        send_y(2, u, so.at[2, u]).start()

    def handle_2(u):
        send_w(2, u, wo.at[1, u]).wait_recv()
        wo[1, u] = tails[head_of(2, u)] + gated(keep(), wr[1, u])
        send_w(3, u, wo.at[1, u]).start()
        send_s(1, u, so.at[1, u]).wait_recv()
        so[1, u] = gated(row(8) == row(10), tails[head_of(1, u)]) + sr[1, u]
        send_s(0, u, so.at[1, u]).start()
        tm[0, u] = so[2, u] + gated(row(7) == row(9), wr[1, u])
        send_t(1, u, tm.at[0, u]).start()
        tm[1, u] = so[1, u] + gated(row(7) == row(10), wr[0, u])
        send_t(2, u, tm.at[1, u]).start()
        send_y(1, u, so.at[1, u]).start()

    def handle_3(u):
        send_w(3, u, wo.at[2, u]).wait_recv()
        wo[2, u] = tails[head_of(3, u)] + gated(keep(), wr[2, u])
        send_t(0, u, wo.at[2, u]).start()
        send_s(0, u, so.at[0, u]).wait_recv()
        so[0, u] = gated(row(8) == row(11), tails[head_of(0, u)]) + sr[0, u]
        send_t(3, u, so.at[0, u]).start()
        send_y(0, u, so.at[0, u]).start()

    @pl.loop(0, heads)
    def _(h):
        for slot, handle in ((H1_SLOT, handle_1), (H2_SLOT, handle_2), (H3_SLOT, handle_3)):
            @pl.when(h == slot)
            def _():
                handle(0)
                handle(1)

        load(0, h).wait()
        qf[h] = feature_map(qraw[h])
        blk = 256
        for b in range(tok // blk):
            rows = pl.ds(b * blk, blk)
            width = (b + 1) * blk
            scores = jnp.dot(qf[h, rows, :], kft[h, :, pl.ds(0, width)], preferred_element_type=F32)
            weights = scores.astype(BF16) * mask[rows, pl.ds(0, width)]
            values = jnp.concatenate([vraw[h, pl.ds(0, width), :], ones_v[:width]], axis=1)
            nd[h, rows, :] = jnp.dot(weights, values, preferred_element_type=F32)

    sqacc[...] = jnp.zeros_like(sqacc)

    def store(h):
        return pltpu.make_async_copy(att.at[h], col(att_hbm, h), out_sem.at[h])

    for p in (1, 2, 0, 3):
        for u in range(heads // 4):
            h = head_of(p, u)
            send_t(p, u, so.at[0, u]).wait_recv()
            send_y(p, u, so.at[0, u]).wait_recv()
            first = df[0:1, :]
            carried = gated(first == row(7 - p), tr[p, u]) + gated(first == row(3 - p), yr[p, u])
            if p:
                carried = carried + gated(first == row(7), wr[p - 1, u])
            norm = jnp.broadcast_to(carried[128:129, :], (128, 128)).T
            both = jnp.concatenate([carried[:128, :], norm], axis=1)
            high = both.astype(BF16)
            low = (both - high.astype(F32)).astype(BF16)
            right = jnp.concatenate([high, low], axis=0)

            @pl.loop(0, tok // 256)
            def _(b):
                rows = pl.ds(pl.multiple_of(b * 256, 256), 256)
                q = qf[h, rows, :] * cmask[rows, :]
                extra = jnp.dot(jnp.concatenate([q, q], axis=1), right, preferred_element_type=F32)
                total = nd[h, rows, :] + extra
                out = total[:, :128] / total[:, 128:]
                att[h, rows, :] = out
                sqacc[rows, :] += out * out

            store(h).start()

    for g in range(groups):
        sq[0, pl.ds(g, 1), :] = jnp.sum(sqacc[pl.ds(g * 128, 128), :].T, axis=0, keepdims=True)

    def send_sq(j):
        return send(sq.at[0], sq.at[j], sq_s.at[j - 1], sq_r.at[j - 1], peer(j))

    for j in range(1, n_head):
        send_sq(j).start()
    for j in range(1, n_head):
        send_sq(j).wait_recv()
    total = jnp.sum(sq[...], axis=0)
    scale = lax.rsqrt(total / n_feat + 1e-06)
    for g in range(groups):
        scale_ref[pl.ds(g * 128, 128), :] = jnp.broadcast_to(scale[g : g + 1, :], (128, 128)).T

    for j in range(1, n_head):
        send_sq(j).wait_send()
    for u in range(heads // 4):
        for p in (1, 2, 3):
            send_w(p, u, wo.at[0, u]).wait_send()
        for p in (0, 1, 2):
            send_s(p, u, so.at[0, u]).wait_send()
        for p in range(4):
            send_y(p, u, so.at[0, u]).wait_send()
            send_t(p, u, so.at[0, u]).wait_send()

    @pl.loop(0, heads)
    def _(h):
        store(h).wait()


def body(n_seq, n_head, query_act, key_act, value_act, norm_gain, doc_lengths):
    tok, width = query_act.shape
    heads = width // E
    two = heads // 4
    any_spec = pl.BlockSpec(memory_space=pl.ANY)
    dma = pltpu.SemaphoreType.DMA
    state = lambda n: pltpu.VMEM((n, two, ROWS, 128), F32)
    att, scale = pl.pallas_call(
        functools.partial(kernel, n_seq, n_head, n_head * width),
        out_shape=(
            jax.ShapeDtypeStruct((tok, width), F32),
            jax.ShapeDtypeStruct((tok, 128), F32),
        ),
        in_specs=[any_spec, any_spec, any_spec, pl.BlockSpec(memory_space=pltpu.SMEM)],
        out_specs=(any_spec, pl.BlockSpec(memory_space=pltpu.VMEM)),
        scratch_shapes=[
            pltpu.VMEM((heads, tok, E), BF16),
            pltpu.VMEM((heads, tok, E), BF16),
            pltpu.VMEM((heads, tok, E), BF16),
            pltpu.VMEM((heads, tok, E), BF16),
            pltpu.VMEM((heads, E, tok), BF16),
            pltpu.VMEM((heads, ROWS, 128), F32),
            pltpu.VMEM((heads, tok, 256), F32),
            pltpu.VMEM((heads, tok, E), F32),
            pltpu.VMEM((tok, 128), F32),
            pltpu.VMEM((tok, tok), BF16),
            pltpu.VMEM((tok, 128), BF16),
            pltpu.VMEM((128, tok), BF16),
            pltpu.VMEM((16, 128), jnp.int32),
            pltpu.VMEM((8, 128), jnp.int32),
            state(3), state(3), state(4), state(4),
            state(3), state(3), state(2),
            pltpu.VMEM((n_head, 8, 128), F32),
            dma((3, heads)), dma((heads,)),
            dma((3, two)), dma((3, two)), dma((3, two)), dma((3, two)),
            dma((4, two)), dma((4, two)), dma((4, two)), dma((4, two)),
            dma((n_head - 1,)), dma((n_head - 1,)),
        ],
        compiler_params=pltpu.CompilerParams(
            collective_id=1, has_side_effects=True, vmem_limit_bytes=48 * 1024 * 1024
        ),
        name="attend",
    )(query_act, key_act, value_act, doc_lengths)
    gain = norm_gain.astype(F32)[None, :]
    return (att * scale[:, 0:1] * gain).astype(BF16)


def solution(mesh):
    in_specs = (P("seq", "head"), P("seq", "head"), P("seq", "head"), P("head"), P())
    fn = functools.partial(body, mesh.shape["seq"], mesh.shape["head"])
    return jax.shard_map(fn, mesh=mesh, in_specs=in_specs, out_specs=P("seq", "head"), check_vma=False)
```

```python
import functools

import jax
import jax.numpy as jnp
from jax import lax
from jax.experimental import pallas as pl
from jax.experimental.pallas import tpu as pltpu
from jax.sharding import PartitionSpec as P

E = 128
ROWS = 136
PARTS = ((0, 136),)
MESH = pl.DeviceIdType.MESH
F32 = jnp.float32
BF16 = jnp.bfloat16


def feature_map(x):
    x = x.astype(F32)
    return jnp.where(x > 0.0, x + 1.0, jnp.exp(x)).astype(BF16)


def kernel(
    n_seq, n_head, n_feat,
    q_hbm, k_hbm, v_hbm, gain_hbm, len_hbm,
    out_hbm,
    qraw, kraw, vraw, qf, kft, tails, nd, att, sqacc,
    mask, cmask, tmask, dl, df,
    len_ref, gain, out, wr, sr, xr, wo, so, xo, car, sq,
    in_sem, small_sem, out_sem,
    wr_s, wr_r, sr_s, sr_r, xr_s, xr_r, sq_s, sq_r,
):
    heads, tok, _ = qraw.shape
    groups = tok // 128
    i = lax.axis_index("seq")
    hd = lax.axis_index("head")

    def shard(d):
        return (lax.rem(i + d + n_seq, n_seq), hd)

    def peer(j):
        return (i, lax.rem(hd + j, n_head))

    def position(j):
        return jnp.where(j < 4, 3 * lax.rem(j, 2), 1 + lax.rem(j, 2))

    def head_of(p, u):
        return lax.rem(i - p + 4 * n_seq, 4) + 4 * u

    def col(ref, h):
        return ref.at[:, pl.ds(pl.multiple_of(h * E, E), E)]

    def load(which, h):
        src, dst = ((q_hbm, qraw), (k_hbm, kraw), (v_hbm, vraw))[which]
        return pltpu.make_async_copy(col(src, h), dst.at[h], in_sem.at[which, h])

    lengths = pltpu.make_async_copy(len_hbm, len_ref, small_sem.at[0])
    gains = pltpu.make_async_copy(gain_hbm, gain, small_sem.at[1])
    lengths.start()
    barrier = pltpu.get_barrier_semaphore()
    senders = [shard(d) for d in (-1, 1, -8, -7)]
    senders += [peer(j) for j in range(1, n_head)]
    for dev in senders:
        pl.semaphore_signal(barrier, inc=1, device_id=dev, device_id_type=MESH)

    @pl.loop(0, heads)
    def _(j):
        h = head_of(position(j), lax.rem(j // 2, 2))
        load(1, h).start()
        load(2, h).start()

    @pl.loop(0, heads)
    def _(h):
        load(0, h).start()

    gains.start()
    lengths.wait()

    base = i * tok
    lane8 = lax.broadcasted_iota(jnp.int32, (8, 128), 1)
    sub8 = lax.broadcasted_iota(jnp.int32, (8, 128), 0)
    sub16 = lax.broadcasted_iota(jnp.int32, (16, 128), 0)
    pos_tok = base + sub8 * 128 + lane8
    pos_last = (i - 7 + sub16) * tok - 1
    pos_first = jnp.zeros((8, 128), jnp.int32) + base
    st_tok = jnp.zeros((8, 128), jnp.int32)
    st_last = jnp.where(pos_last < 0, -1, 0)
    st_first = jnp.zeros((8, 128), jnp.int32)
    end = jnp.int32(0)
    for d in range(len_ref.shape[0]):
        end = end + len_ref[d]
        st_tok = jnp.where(pos_tok >= end, end, st_tok)
        st_last = jnp.where(pos_last >= end, end, st_last)
        st_first = jnp.where(pos_first >= end, end, st_first)
    dl[...] = st_last
    df[...] = st_first

    lane = lax.broadcasted_iota(jnp.int32, (128, 128), 1).astype(F32)
    sub = lax.broadcasted_iota(jnp.int32, (128, 128), 0).astype(F32)
    st_loc = (st_tok - base).astype(F32)
    tail_start = (st_last[8:9, :] - base).astype(F32)
    one, zero = jnp.ones((128, 128), F32), jnp.zeros((128, 128), F32)
    for g in range(groups):
        rows = pl.ds(g * 128, 128)
        tmask[:, rows] = jnp.where(lane + 128.0 * g >= tail_start, one, zero).astype(BF16)

    pl.semaphore_wait(barrier, len(senders))

    ones_v = jnp.ones((tok, 128), BF16)

    def send(src, dst, s_sem, r_sem, dev):
        return pltpu.make_async_remote_copy(
            src_ref=src, dst_ref=dst, send_sem=s_sem, recv_sem=r_sem, device_id=dev, device_id_type=MESH
        )

    def part(ref, c):
        return ref.at[pl.ds(*PARTS[c]), :]

    def send_w(p, u, c, src):
        w = (p - 1, u, c)
        return send(part(src, c), part(wr.at[p - 1, u], c), wr_s.at[w], wr_r.at[w], shard(1))

    def send_s(p, u, c, src):
        w = (p, u, c)
        return send(part(src, c), part(sr.at[p, u], c), sr_s.at[w], sr_r.at[w], shard(-1))

    def send_x(kind, u, c, src):
        dist = (7, -1, 1, 1, 8, 8)[kind]
        w = (kind, u, c)
        return send(part(src, c), part(xr.at[kind, u], c), xr_s.at[w], xr_r.at[w], shard(dist))

    splits = range(len(PARTS))

    @pl.loop(0, heads)
    def _(j):
        p = position(j)
        u = lax.rem(j // 2, 2)
        h = head_of(p, u)
        load(1, h).wait()
        kt = feature_map(kraw[h]).T
        kft[h] = kt
        load(2, h).wait()
        state = jnp.dot(
            kt * tmask[...],
            jnp.concatenate([vraw[h], ones_v], axis=1),
            preferred_element_type=F32,
        )
        tails[h, pl.ds(0, 128), :] = state[:, :128]
        tails[h, pl.ds(128, 8), :] = state[:, 128:].T[0:8, :]

        @pl.when((j < 4) & (p == 0))
        def _():
            for c in splits:
                send_w(1, u, c, tails.at[h]).start()

        @pl.when((j < 4) & (p == 3))
        def _():
            for c in splits:
                send_s(2, u, c, tails.at[h]).start()

    for g in range(groups):
        first = jnp.broadcast_to(st_loc[g : g + 1, :], (128, 128)).T
        rows = pl.ds(g * 128, 128)
        cmask[rows, :] = jnp.where(first <= 0.0, one, zero).astype(BF16)
        for k in range(2 * (g // 2) + 2):
            s = lane + 128.0 * k
            keep = s >= first
            if k == g:
                keep = keep & (lane <= sub)
            value = jnp.where(keep, one, zero) if k <= g else zero
            mask[rows, pl.ds(k * 128, 128)] = value.astype(BF16)

    def row(r):
        return dl[pl.ds(r, 1), :]

    def gated(cond, x):
        return jnp.where(cond, x, 0.0)

    first = df[0:1, :]

    def prefix(p, u, c):
        rows = pl.ds(*PARTS[c])
        send_w(p, u, c, wo.at[p - 1, u]).wait_recv()
        wo[p - 1, u, rows] = tails[head_of(p, u), rows] + gated(row(8) == row(7), wr[p - 1, u, rows])
        if p < 3:
            send_w(p + 1, u, c, wo.at[p - 1, u]).start()

    def suffix(p, u, c):
        rows = pl.ds(*PARTS[c])
        send_s(p, u, c, so.at[p, u]).wait_recv()
        so[p, u, rows] = gated(row(8) == row(11 - p), tails[head_of(p, u), rows]) + sr[p, u, rows]
        if p:
            send_s(p - 1, u, c, so.at[p, u]).start()
        else:
            send_x(0, u, c, so.at[0, u]).start()

    wrapped = lax.rem(i, n_seq // 4) == 0

    def step(p, u):
        @pl.when(wrapped)
        def _():
            for c in splits:
                suffix(3 - p, u, c)
                prefix(p, u, c)

        @pl.when(jnp.logical_not(wrapped))
        def _():
            for c in splits:
                prefix(p, u, c)
                suffix(3 - p, u, c)

    def handle_4(u):
        for c in splits:
            rows = pl.ds(*PARTS[c])
            send_x(0, u, c, so.at[0, u]).wait_recv()
            send_x(1, u, c, xr.at[0, u]).start()
            xo[0, u, rows] = wo[2, u, rows] + gated(row(8) == row(4), xr[0, u, rows])
            send_x(2, u, c, xo.at[0, u]).start()

    def handle_5(u):
        for c in splits:
            rows = pl.ds(*PARTS[c])
            send_x(2, u, c, xo.at[0, u]).wait_recv()
            carried = gated(first == row(7), xr[2, u, rows])
            car[0, u, rows] = carried
            xo[1, u, rows] = tails[head_of(0, u), rows] + gated(row(8) == first, carried)
            send_x(3, u, c, xo.at[1, u]).start()

    def last_3(u):
        for c in splits:
            send_x(4, u, c, so.at[0, u]).wait_recv()
        car[3, u] = (
            gated(first == row(7), wr[2, u])
            + gated(first == row(4), xr[0, u])
            + gated(first == row(0), xr[4, u])
        )

    def last_2(u):
        for c in splits:
            send_x(1, u, c, so.at[0, u]).wait_recv()
            send_x(5, u, c, so.at[0, u]).wait_recv()
        car[2, u] = (
            gated(first == row(7), wr[1, u])
            + gated(first == row(5), xr[1, u])
            + gated(first == row(1), xr[5, u])
        )

    def last_1(u):
        for c in splits:
            send_x(3, u, c, so.at[0, u]).wait_recv()
        car[1, u] = gated(first == row(7), xr[3, u])

    @pl.loop(0, heads)
    def _(h):
        for p in (1, 2, 3):
            @pl.when(h // 2 == p - 1)
            def _():
                step(p, lax.rem(h, 2))

        @pl.when((h == 1) | (h == 2))
        def _():
            for c in splits:
                send_x(4, h - 1, c, tails.at[head_of(3, h - 1)]).start()

        @pl.when((h == 3) | (h == 4))
        def _():
            for c in splits:
                send_x(5, h - 3, c, so.at[2, h - 3]).start()

        @pl.when(h // 2 == 3)
        def _():
            handle_4(lax.rem(h, 2))

        load(0, h).wait()
        qf[h] = feature_map(qraw[h])
        blk = 256
        for b in range(tok // blk):
            rows = pl.ds(b * blk, blk)
            width = (b + 1) * blk
            scores = jnp.dot(qf[h, rows, :], kft[h, :, pl.ds(0, width)], preferred_element_type=F32)
            weights = scores.astype(BF16) * mask[rows, pl.ds(0, width)]
            values = jnp.concatenate([vraw[h, pl.ds(0, width), :], ones_v[:width]], axis=1)
            nd[h, rows, :] = jnp.dot(weights, values, preferred_element_type=F32)

    sqacc[...] = jnp.zeros_like(sqacc)

    def finish(p, u):
        h = head_of(p, u)
        carried = car[p, u]
        norm = jnp.broadcast_to(carried[128:129, :], (128, 128)).T
        both = jnp.concatenate([carried[:128, :], norm], axis=1)
        high = both.astype(BF16)
        low = (both - high.astype(F32)).astype(BF16)
        right = jnp.concatenate([high, low], axis=0)

        for b in range(tok // 256):
            rows = pl.ds(b * 256, 256)
            q = qf[h, rows, :] * cmask[rows, :]
            extra = jnp.dot(jnp.concatenate([q, q], axis=1), right, preferred_element_type=F32)
            total = nd[h, rows, :] + extra
            result = total[:, :128] / total[:, 128:]
            att[h, rows, :] = result
            sqacc[rows, :] += result * result

    last_3(0)
    finish(3, 0)
    handle_5(0)
    last_3(1)
    finish(3, 1)
    handle_5(1)
    finish(0, 0)
    last_2(0)
    finish(2, 0)
    finish(0, 1)
    last_2(1)
    finish(2, 1)
    last_1(0)
    finish(1, 0)
    last_1(1)
    finish(1, 1)

    for g in range(groups):
        sq[0, pl.ds(g, 1), :] = jnp.sum(sqacc[pl.ds(g * 128, 128), :].T, axis=0, keepdims=True)

    def send_sq(j):
        return send(sq.at[0], sq.at[j], sq_s.at[j - 1], sq_r.at[j - 1], peer(j))

    for j in range(1, n_head):
        send_sq(j).start()
    for j in range(1, n_head):
        send_sq(j).wait_recv()
    total = jnp.sum(sq[...], axis=0)
    scale = lax.rsqrt(total / n_feat + 1e-06)
    gains.wait()

    def store(g):
        rows = pl.ds(g * 128, 128)
        return pltpu.make_async_copy(out.at[rows, :], out_hbm.at[rows, :], out_sem.at[g])

    for g in range(groups):
        rows = pl.ds(g * 128, 128)
        factor = jnp.broadcast_to(scale[g : g + 1, :], (128, 128)).T
        for h in range(heads):
            cols = pl.ds(h * E, E)
            weight = gain[cols].astype(F32)[None, :]
            out[rows, cols] = (att[h, rows, :] * factor * weight).astype(BF16)
        store(g).start()

    for j in range(1, n_head):
        send_sq(j).wait_send()
    for u in range(heads // 4):
        for c in splits:
            for p in (1, 2, 3):
                send_w(p, u, c, wo.at[0, u]).wait_send()
            for p in (0, 1, 2):
                send_s(p, u, c, so.at[0, u]).wait_send()
            for kind in range(6):
                send_x(kind, u, c, xo.at[0, u]).wait_send()
    for g in range(groups):
        store(g).wait()


def body(n_seq, n_head, query_act, key_act, value_act, norm_gain, doc_lengths):
    tok, width = query_act.shape
    heads = width // E
    two = heads // 4
    any_spec = pl.BlockSpec(memory_space=pl.ANY)
    dma = pltpu.SemaphoreType.DMA
    state = lambda n: pltpu.VMEM((n, two, ROWS, 128), F32)
    arrivals = lambda n: dma((n, two, len(PARTS)))
    return pl.pallas_call(
        functools.partial(kernel, n_seq, n_head, n_head * width),
        out_shape=jax.ShapeDtypeStruct((tok, width), BF16),
        in_specs=[any_spec] * 5,
        out_specs=any_spec,
        scratch_shapes=[
            pltpu.VMEM((heads, tok, E), BF16),
            pltpu.VMEM((heads, tok, E), BF16),
            pltpu.VMEM((heads, tok, E), BF16),
            pltpu.VMEM((heads, tok, E), BF16),
            pltpu.VMEM((heads, E, tok), BF16),
            pltpu.VMEM((heads, ROWS, 128), F32),
            pltpu.VMEM((heads, tok, 256), F32),
            pltpu.VMEM((heads, tok, E), F32),
            pltpu.VMEM((tok, 128), F32),
            pltpu.VMEM((tok, tok), BF16),
            pltpu.VMEM((tok, 128), BF16),
            pltpu.VMEM((128, tok), BF16),
            pltpu.VMEM((16, 128), jnp.int32),
            pltpu.VMEM((8, 128), jnp.int32),
            pltpu.SMEM(doc_lengths.shape, jnp.int32),
            pltpu.VMEM((width,), BF16),
            pltpu.VMEM((tok, width), BF16),
            state(3), state(3), state(6),
            state(3), state(3), state(2), state(4),
            pltpu.VMEM((n_head, 8, 128), F32),
            dma((3, heads)), dma((2,)), dma((tok // 128,)),
            arrivals(3), arrivals(3), arrivals(3), arrivals(3),
            arrivals(6), arrivals(6),
            dma((n_head - 1,)), dma((n_head - 1,)),
        ],
        compiler_params=pltpu.CompilerParams(
            collective_id=1, has_side_effects=True, vmem_limit_bytes=62 * 1024 * 1024
        ),
        name="attend",
    )(query_act, key_act, value_act, norm_gain, doc_lengths)


def solution(mesh):
    in_specs = (P("seq", "head"), P("seq", "head"), P("seq", "head"), P("head"), P())
    fn = functools.partial(body, mesh.shape["seq"], mesh.shape["head"])
    return jax.shard_map(fn, mesh=mesh, in_specs=in_specs, out_specs=P("seq", "head"), check_vma=False)
```

```python
import functools

import jax
import jax.numpy as jnp
from jax import lax
from jax.experimental import pallas as pl
from jax.experimental.pallas import tpu as pltpu
from jax.sharding import PartitionSpec as P

E = 128
ROWS = 136
PARTS = ((0, 136),)
SLOTS = ((0, 0, 0), (1, 1, 0), (3, 0, 1), (4, 1, 1), (6, 0, 2), (7, 1, 2))
MESH = pl.DeviceIdType.MESH
F32 = jnp.float32
BF16 = jnp.bfloat16


def feature_map(x):
    x = x.astype(F32)
    return jnp.where(x > 0.0, x + 1.0, jnp.exp(x)).astype(BF16)


def kernel(
    n_seq, n_head, n_feat,
    q_hbm, k_hbm, v_hbm, gain_hbm, len_hbm,
    out,
    qraw, kraw, vraw, qf, kft, tails, nd, att, sqacc,
    mask, cmask, tmask, dl, df,
    len_ref, gain, wr, sr, xr, wo, so, xo, car, sq,
    in_sem, small_sem,
    rl, rl_s, rl_r, wr_s, wr_r, sr_s, sr_r, xr_s, xr_r, sq_s, sq_r,
):
    heads, tok, _ = qraw.shape
    groups = tok // 128
    i = lax.axis_index("seq")
    hd = lax.axis_index("head")

    wrapped = lax.rem(i, n_seq // 4) == 0
    over = jnp.where(wrapped, -8, 8)

    def shard(d):
        return (lax.rem(i + d + n_seq, n_seq), hd)

    def peer(j):
        return (i, lax.rem(hd + j, n_head))

    def position(j):
        return jnp.where(j < 4, 3 * lax.rem(j, 2), 1 + lax.rem(j, 2))

    def head_of(p, u):
        return lax.rem(i - p + 4 * n_seq, 4) + 4 * u

    def col(ref, h):
        return ref.at[:, pl.ds(pl.multiple_of(h * E, E), E)]

    def load(which, h):
        src, dst = ((q_hbm, qraw), (k_hbm, kraw), (v_hbm, vraw))[which]
        return pltpu.make_async_copy(col(src, h), dst.at[h], in_sem.at[which, h])

    lengths = pltpu.make_async_copy(len_hbm, len_ref, small_sem.at[0])
    gains = pltpu.make_async_copy(gain_hbm, gain, small_sem.at[1])
    lengths.start()
    barrier = pltpu.get_barrier_semaphore()
    senders = [shard(d) for d in (-1, 1, -over, -7)]
    senders += [peer(j) for j in range(1, n_head)]
    for dev in senders:
        pl.semaphore_signal(barrier, inc=1, device_id=dev, device_id_type=MESH)

    @pl.loop(0, heads)
    def _(j):
        h = head_of(position(j), lax.rem(j // 2, 2))
        load(1, h).start()
        load(2, h).start()

    @pl.loop(0, heads)
    def _(h):
        load(0, h).start()

    gains.start()
    lengths.wait()

    base = i * tok
    lane8 = lax.broadcasted_iota(jnp.int32, (8, 128), 1)
    sub8 = lax.broadcasted_iota(jnp.int32, (8, 128), 0)
    sub16 = lax.broadcasted_iota(jnp.int32, (16, 128), 0)
    pos_tok = base + sub8 * 128 + lane8
    pos_last = (i - 7 + sub16) * tok - 1
    pos_first = jnp.zeros((8, 128), jnp.int32) + base
    st_tok = jnp.zeros((8, 128), jnp.int32)
    st_last = jnp.where(pos_last < 0, -1, 0)
    st_first = jnp.zeros((8, 128), jnp.int32)
    end = jnp.int32(0)
    for d in range(len_ref.shape[0]):
        end = end + len_ref[d]
        st_tok = jnp.where(pos_tok >= end, end, st_tok)
        st_last = jnp.where(pos_last >= end, end, st_last)
        st_first = jnp.where(pos_first >= end, end, st_first)
    dl[...] = st_last
    df[...] = st_first

    lane = lax.broadcasted_iota(jnp.int32, (128, 128), 1).astype(F32)
    sub = lax.broadcasted_iota(jnp.int32, (128, 128), 0).astype(F32)
    st_loc = (st_tok - base).astype(F32)
    tail_start = (st_last[8:9, :] - base).astype(F32)
    one, zero = jnp.ones((128, 128), F32), jnp.zeros((128, 128), F32)
    for g in range(groups):
        rows = pl.ds(g * 128, 128)
        tmask[:, rows] = jnp.where(lane + 128.0 * g >= tail_start, one, zero).astype(BF16)

    pl.semaphore_wait(barrier, len(senders))

    ones_v = jnp.ones((tok, 128), BF16)

    def send(src, dst, s_sem, r_sem, dev):
        return pltpu.make_async_remote_copy(
            src_ref=src, dst_ref=dst, send_sem=s_sem, recv_sem=r_sem, device_id=dev, device_id_type=MESH
        )

    def part(ref, c):
        return ref.at[pl.ds(*PARTS[c]), :]

    def send_w(p, u, c, src):
        w = (p - 1, u, c)
        return send(part(src, c), part(wr.at[p - 1, u], c), wr_s.at[w], wr_r.at[w], shard(1))

    def send_s(p, u, c, src):
        w = (p, u, c)
        return send(part(src, c), part(sr.at[p, u], c), sr_s.at[w], sr_r.at[w], shard(-1))

    def send_x(kind, u, c, src):
        dist = (7, -1, 1, 1, over, over)[kind]
        w = (kind, u, c)
        return send(part(src, c), part(xr.at[kind, u], c), xr_s.at[w], xr_r.at[w], shard(dist))

    splits = range(len(PARTS))

    def send_relay(stage, kind, u, c, src):
        w = (stage, kind, u, c)
        return send(part(src, c), part(rl.at[stage, kind, u], c), rl_s.at[w], rl_r.at[w], shard(over))

    def suffix_over(stage, kind, u, here):
        own = tails.at[head_of(3, u)] if kind == 0 else so.at[2, u]
        for c in splits:
            if not here:
                send_x(4 + kind, u, c, own).start()
            elif stage == 0:
                send_relay(0, kind, u, c, own).start()
            else:
                send_relay(stage - 1, kind, u, c, own).wait_recv()
                src = rl.at[stage - 1, kind, u]
                (send_relay(1, kind, u, c, src) if stage == 1 else send_x(4 + kind, u, c, src)).start()

    @pl.loop(0, heads)
    def _(j):
        p = position(j)
        u = lax.rem(j // 2, 2)
        h = head_of(p, u)
        load(1, h).wait()
        kt = feature_map(kraw[h]).T
        kft[h] = kt
        load(2, h).wait()
        state = jnp.dot(
            kt * tmask[...],
            jnp.concatenate([vraw[h], ones_v], axis=1),
            preferred_element_type=F32,
        )
        tails[h, pl.ds(0, 128), :] = state[:, :128]
        tails[h, pl.ds(128, 8), :] = state[:, 128:].T[0:8, :]

        @pl.when((j < 4) & (p == 0))
        def _():
            for c in splits:
                send_w(1, u, c, tails.at[h]).start()

        @pl.when((j < 4) & (p == 3))
        def _():
            for c in splits:
                send_s(2, u, c, tails.at[h]).start()

    for g in range(groups):
        first = jnp.broadcast_to(st_loc[g : g + 1, :], (128, 128)).T
        rows = pl.ds(g * 128, 128)
        cmask[rows, :] = jnp.where(first <= 0.0, one, zero).astype(BF16)
        for k in range(2 * (g // 2) + 2):
            s = lane + 128.0 * k
            keep = s >= first
            if k == g:
                keep = keep & (lane <= sub)
            value = jnp.where(keep, one, zero) if k <= g else zero
            mask[rows, pl.ds(k * 128, 128)] = value.astype(BF16)

    def row(r):
        return dl[pl.ds(r, 1), :]

    def gated(cond, x):
        return jnp.where(cond, x, 0.0)

    first = df[0:1, :]

    def prefix(p, u, c):
        rows = pl.ds(*PARTS[c])
        send_w(p, u, c, wo.at[p - 1, u]).wait_recv()
        wo[p - 1, u, rows] = tails[head_of(p, u), rows] + gated(row(8) == row(7), wr[p - 1, u, rows])
        if p < 3:
            send_w(p + 1, u, c, wo.at[p - 1, u]).start()

    def suffix(p, u, c):
        rows = pl.ds(*PARTS[c])
        send_s(p, u, c, so.at[p, u]).wait_recv()
        so[p, u, rows] = gated(row(8) == row(11 - p), tails[head_of(p, u), rows]) + sr[p, u, rows]
        if p:
            send_s(p - 1, u, c, so.at[p, u]).start()
        else:
            send_x(0, u, c, so.at[0, u]).start()

    def step(p, u):
        @pl.when(wrapped)
        def _():
            for c in splits:
                suffix(3 - p, u, c)
                prefix(p, u, c)

        @pl.when(lax.rem(i, n_seq // 4) != 0)
        def _():
            for c in splits:
                prefix(p, u, c)
                suffix(3 - p, u, c)

    def handle_4(u):
        for c in splits:
            rows = pl.ds(*PARTS[c])
            send_x(0, u, c, so.at[0, u]).wait_recv()
            send_x(1, u, c, xr.at[0, u]).start()
            xo[0, u, rows] = wo[2, u, rows] + gated(row(8) == row(4), xr[0, u, rows])
            send_x(2, u, c, xo.at[0, u]).start()

    def handle_5(u):
        for c in splits:
            rows = pl.ds(*PARTS[c])
            send_x(2, u, c, xo.at[0, u]).wait_recv()
            carried = gated(first == row(7), xr[2, u, rows])
            car[0, u, rows] = carried
            xo[1, u, rows] = tails[head_of(0, u), rows] + gated(row(8) == first, carried)
            send_x(3, u, c, xo.at[1, u]).start()

    def last_3(u):
        for c in splits:
            send_x(4, u, c, so.at[0, u]).wait_recv()
        car[3, u] = (
            gated(first == row(7), wr[2, u])
            + gated(first == row(4), xr[0, u])
            + gated(first == row(0), xr[4, u])
        )

    def last_2(u):
        for c in splits:
            send_x(1, u, c, so.at[0, u]).wait_recv()
            send_x(5, u, c, so.at[0, u]).wait_recv()
        car[2, u] = (
            gated(first == row(7), wr[1, u])
            + gated(first == row(5), xr[1, u])
            + gated(first == row(1), xr[5, u])
        )

    def last_1(u):
        for c in splits:
            send_x(3, u, c, so.at[0, u]).wait_recv()
        car[1, u] = gated(first == row(7), xr[3, u])

    @pl.loop(0, heads)
    def _(h):
        for p in (1, 2, 3):
            @pl.when(h // 2 == p - 1)
            def _():
                step(p, lax.rem(h, 2))

        v = lax.rem(h, 2)
        for slot, kind, stage in SLOTS:
            @pl.when((h == slot) & (lax.rem(i, n_seq // 4) == 0))
            def _():
                for u in range(2):
                    suffix_over(stage, kind, u, True)

            if stage == 0:
                @pl.when((h == slot) & (lax.rem(i, n_seq // 4) != 0))
                def _():
                    for u in range(2):
                        suffix_over(stage, kind, u, False)

        @pl.when(h // 2 == 3)
        def _():
            handle_4(lax.rem(h, 2))

        load(0, h).wait()
        qf[h] = feature_map(qraw[h])
        blk = 256
        for b in range(tok // blk):
            rows = pl.ds(b * blk, blk)
            width = (b + 1) * blk
            scores = jnp.dot(qf[h, rows, :], kft[h, :, pl.ds(0, width)], preferred_element_type=F32)
            weights = scores.astype(BF16) * mask[rows, pl.ds(0, width)]
            values = jnp.concatenate([vraw[h, pl.ds(0, width), :], ones_v[:width]], axis=1)
            nd[h, rows, :] = jnp.dot(weights, values, preferred_element_type=F32)

    sqacc[...] = jnp.zeros_like(sqacc)

    def finish(p, u):
        h = head_of(p, u)
        carried = car[p, u]
        norm = jnp.broadcast_to(carried[128:129, :], (128, 128)).T
        both = jnp.concatenate([carried[:128, :], norm], axis=1)
        high = both.astype(BF16)
        low = (both - high.astype(F32)).astype(BF16)
        right = jnp.concatenate([high, low], axis=0)

        for b in range(tok // 256):
            rows = pl.ds(b * 256, 256)
            q = qf[h, rows, :] * cmask[rows, :]
            extra = jnp.dot(jnp.concatenate([q, q], axis=1), right, preferred_element_type=F32)
            total = nd[h, rows, :] + extra
            result = total[:, :128] / total[:, 128:]
            att[h, rows, :] = result
            sqacc[rows, :] += result * result

    last_3(0)
    finish(3, 0)
    handle_5(0)
    last_3(1)
    finish(3, 1)
    handle_5(1)
    finish(0, 0)
    last_2(0)
    finish(2, 0)
    finish(0, 1)
    last_2(1)
    finish(2, 1)
    last_1(0)
    finish(1, 0)
    last_1(1)
    finish(1, 1)

    for g in range(groups):
        sq[0, pl.ds(g, 1), :] = jnp.sum(sqacc[pl.ds(g * 128, 128), :].T, axis=0, keepdims=True)

    def send_sq(j):
        return send(sq.at[0], sq.at[j], sq_s.at[j - 1], sq_r.at[j - 1], peer(j))

    for j in range(1, n_head):
        send_sq(j).start()
    for j in range(1, n_head):
        send_sq(j).wait_recv()
    total = jnp.sum(sq[...], axis=0)
    scale = lax.rsqrt(total / n_feat + 1e-06)
    gains.wait()

    for g in range(groups):
        rows = pl.ds(g * 128, 128)
        factor = jnp.broadcast_to(scale[g : g + 1, :], (128, 128)).T
        for h in range(heads):
            cols = pl.ds(h * E, E)
            weight = gain[cols].astype(F32)[None, :]
            out[rows, cols] = (att[h, rows, :] * factor * weight).astype(BF16)

    for j in range(1, n_head):
        send_sq(j).wait_send()
    @pl.when(wrapped)
    def _():
        for u in range(heads // 4):
            for c in splits:
                for stage in (0, 1):
                    for kind in (0, 1):
                        send_relay(stage, kind, u, c, xo.at[0, u]).wait_send()

    for u in range(heads // 4):
        for c in splits:
            for p in (1, 2, 3):
                send_w(p, u, c, wo.at[0, u]).wait_send()
            for p in (0, 1, 2):
                send_s(p, u, c, so.at[0, u]).wait_send()
            for kind in range(6):
                send_x(kind, u, c, xo.at[0, u]).wait_send()


def body(n_seq, n_head, query_act, key_act, value_act, norm_gain, doc_lengths):
    tok, width = query_act.shape
    heads = width // E
    two = heads // 4
    any_spec = pl.BlockSpec(memory_space=pl.ANY)
    dma = pltpu.SemaphoreType.DMA
    state = lambda n: pltpu.VMEM((n, two, ROWS, 128), F32)
    arrivals = lambda n: dma((n, two, len(PARTS)))
    return pl.pallas_call(
        functools.partial(kernel, n_seq, n_head, n_head * width),
        out_shape=pltpu.VMEM((tok, width), BF16),
        in_specs=[any_spec] * 5,
        out_specs=pl.BlockSpec(memory_space=pltpu.VMEM),
        scratch_shapes=[
            pltpu.VMEM((heads, tok, E), BF16),
            pltpu.VMEM((heads, tok, E), BF16),
            pltpu.VMEM((heads, tok, E), BF16),
            pltpu.VMEM((heads, tok, E), BF16),
            pltpu.VMEM((heads, E, tok), BF16),
            pltpu.VMEM((heads, ROWS, 128), F32),
            pltpu.VMEM((heads, tok, 256), F32),
            pltpu.VMEM((heads, tok, E), F32),
            pltpu.VMEM((tok, 128), F32),
            pltpu.VMEM((tok, tok), BF16),
            pltpu.VMEM((tok, 128), BF16),
            pltpu.VMEM((128, tok), BF16),
            pltpu.VMEM((16, 128), jnp.int32),
            pltpu.VMEM((8, 128), jnp.int32),
            pltpu.SMEM(doc_lengths.shape, jnp.int32),
            pltpu.VMEM((width,), BF16),
            state(3), state(3), state(6),
            state(3), state(3), state(2), state(4),
            pltpu.VMEM((n_head, 8, 128), F32),
            dma((3, heads)), dma((2,)),
            pltpu.VMEM((2, 2, two, ROWS, 128), F32),
            dma((2, 2, two, len(PARTS))), dma((2, 2, two, len(PARTS))),
            arrivals(3), arrivals(3), arrivals(3), arrivals(3),
            arrivals(6), arrivals(6),
            dma((n_head - 1,)), dma((n_head - 1,)),
        ],
        compiler_params=pltpu.CompilerParams(
            collective_id=1, has_side_effects=True, vmem_limit_bytes=56 * 1024 * 1024
        ),
        name="attend",
    )(query_act, key_act, value_act, norm_gain, doc_lengths)


def solution(mesh):
    in_specs = (P("seq", "head"), P("seq", "head"), P("seq", "head"), P("head"), P())
    fn = functools.partial(body, mesh.shape["seq"], mesh.shape["head"])
    return jax.shard_map(fn, mesh=mesh, in_specs=in_specs, out_specs=P("seq", "head"), check_vma=False)
```

```python
import functools

import jax
import jax.numpy as jnp
from jax import lax
from jax.experimental import pallas as pl
from jax.experimental.pallas import tpu as pltpu
from jax.sharding import PartitionSpec as P

E = 128
ROWS = 136
PARTS = ((0, 129),)
SENT = 129
SLOTS = ((0, 0, 0), (1, 1, 0), (3, 0, 1), (4, 1, 1), (6, 0, 2), (7, 1, 2))
MESH = pl.DeviceIdType.MESH
F32 = jnp.float32
BF16 = jnp.bfloat16


def feature_map(x):
    x = x.astype(F32)
    return jnp.where(x > 0.0, x + 1.0, jnp.exp(x)).astype(BF16)


def kernel(
    n_seq, n_head, n_feat,
    q_hbm, k_hbm, v_hbm, gain_hbm, len_hbm,
    out,
    qraw, kraw, vraw, qf, kft, tails, nd, att, sqacc,
    mask, cmask, tmask, dl, df,
    len_ref, gain, wr, sr, xr, wo, so, xo, car, sq,
    in_sem, small_sem,
    rl, rl_s, rl_r, wr_s, wr_r, sr_s, sr_r, xr_s, xr_r, sq_s, sq_r,
):
    heads, tok, _ = qraw.shape
    groups = tok // 128
    i = lax.axis_index("seq")
    hd = lax.axis_index("head")

    n_z = 8
    z = lax.rem(i, n_z)
    wrapped = z == 0
    over = jnp.where(wrapped, -8, 8)

    def shard(d):
        return (lax.rem(i + d + n_seq, n_seq), hd)

    def peer(j):
        return (i, lax.rem(hd + j, n_head))

    def position(j):
        return jnp.where(j < 4, 3 * lax.rem(j, 2), 1 + lax.rem(j, 2))

    def head_of(p, u):
        return lax.rem(i - p + 4 * n_seq, 4) + 4 * u

    def col(ref, h):
        return ref.at[:, pl.ds(pl.multiple_of(h * E, E), E)]

    def load(which, h):
        src, dst = ((q_hbm, qraw), (k_hbm, kraw), (v_hbm, vraw))[which]
        return pltpu.make_async_copy(col(src, h), dst.at[h], in_sem.at[which, h])

    lengths = pltpu.make_async_copy(len_hbm, len_ref, small_sem.at[0])
    gains = pltpu.make_async_copy(gain_hbm, gain, small_sem.at[1])
    lengths.start()
    barrier = pltpu.get_barrier_semaphore()
    senders = [shard(d) for d in (-1, 1, -over, -7)]
    senders += [peer(j) for j in range(1, n_head)]
    for dev in senders:
        pl.semaphore_signal(barrier, inc=1, device_id=dev, device_id_type=MESH)

    @pl.when(z == 1)
    def _():
        pl.semaphore_signal(barrier, inc=1, device_id=shard(-2), device_id_type=MESH)

    @pl.loop(0, heads)
    def _(j):
        h = head_of(position(j), lax.rem(j // 2, 2))
        load(1, h).start()
        load(2, h).start()

    @pl.loop(0, heads)
    def _(h):
        load(0, h).start()

    gains.start()
    lengths.wait()

    base = i * tok
    lane8 = lax.broadcasted_iota(jnp.int32, (8, 128), 1)
    sub8 = lax.broadcasted_iota(jnp.int32, (8, 128), 0)
    sub16 = lax.broadcasted_iota(jnp.int32, (16, 128), 0)
    pos_tok = base + sub8 * 128 + lane8
    pos_last = (i - 7 + sub16) * tok - 1
    pos_first = jnp.zeros((8, 128), jnp.int32) + base
    st_tok = jnp.zeros((8, 128), jnp.int32)
    st_last = jnp.where(pos_last < 0, -1, 0)
    st_first = jnp.zeros((8, 128), jnp.int32)
    end = jnp.int32(0)
    for d in range(len_ref.shape[0]):
        end = end + len_ref[d]
        st_tok = jnp.where(pos_tok >= end, end, st_tok)
        st_last = jnp.where(pos_last >= end, end, st_last)
        st_first = jnp.where(pos_first >= end, end, st_first)
    dl[...] = st_last
    df[...] = st_first

    lane = lax.broadcasted_iota(jnp.int32, (128, 128), 1).astype(F32)
    sub = lax.broadcasted_iota(jnp.int32, (128, 128), 0).astype(F32)
    st_loc = (st_tok - base).astype(F32)
    tail_start = (st_last[8:9, :] - base).astype(F32)
    one, zero = jnp.ones((128, 128), F32), jnp.zeros((128, 128), F32)
    for g in range(groups):
        rows = pl.ds(g * 128, 128)
        tmask[:, rows] = jnp.where(lane + 128.0 * g >= tail_start, one, zero).astype(BF16)

    pl.semaphore_wait(barrier, len(senders) + jnp.where(z == n_z - 1, 1, 0))

    ones_v = jnp.ones((tok, 128), BF16)

    def send(src, dst, s_sem, r_sem, dev):
        return pltpu.make_async_remote_copy(
            src_ref=src, dst_ref=dst, send_sem=s_sem, recv_sem=r_sem, device_id=dev, device_id_type=MESH
        )

    def part(ref, c):
        return ref.at[pl.ds(*PARTS[c]), :]

    def send_w(p, u, c, src):
        w = (p - 1, u, c)
        return send(part(src, c), part(wr.at[p - 1, u], c), wr_s.at[w], wr_r.at[w], shard(1))

    def send_s(p, u, c, src):
        w = (p, u, c)
        return send(part(src, c), part(sr.at[p, u], c), sr_s.at[w], sr_r.at[w], shard(-1))

    def send_x(kind, u, c, src):
        dist = (7, -1, 1, 1, over, over, 8, 2)[kind]
        w = (kind, u, c)
        return send(part(src, c), part(xr.at[kind, u], c), xr_s.at[w], xr_r.at[w], shard(dist))

    splits = range(len(PARTS))

    def send_relay(stage, kind, u, c, src):
        w = (stage, kind, u, c)
        return send(part(src, c), part(rl.at[stage, kind, u], c), rl_s.at[w], rl_r.at[w], shard(over))

    def suffix_over(stage, kind, u, here):
        own = tails.at[head_of(3, u)] if kind == 0 else so.at[2, u]
        for c in splits:
            if not here:
                send_x(4 + kind, u, c, own).start()
            elif stage == 0:
                send_relay(0, kind, u, c, own).start()
            else:
                send_relay(stage - 1, kind, u, c, own).wait_recv()
                src = rl.at[stage - 1, kind, u]
                (send_relay(1, kind, u, c, src) if stage == 1 else send_x(4 + kind, u, c, src)).start()

    @pl.loop(0, heads)
    def _(j):
        p = position(j)
        u = lax.rem(j // 2, 2)
        h = head_of(p, u)
        load(1, h).wait()
        kt = feature_map(kraw[h]).T
        kft[h] = kt
        load(2, h).wait()
        state = jnp.dot(
            kt * tmask[...],
            jnp.concatenate([vraw[h], ones_v], axis=1),
            preferred_element_type=F32,
        )
        tails[h, pl.ds(0, 128), :] = state[:, :128]
        tails[h, pl.ds(128, 8), :] = state[:, 128:].T[0:8, :]

        @pl.when((j < 4) & (p == 0))
        def _():
            for c in splits:
                send_w(1, u, c, tails.at[h]).start()

        @pl.when((j < 4) & (p == 3))
        def _():
            for c in splits:
                send_s(2, u, c, tails.at[h]).start()

    for g in range(groups):
        first = jnp.broadcast_to(st_loc[g : g + 1, :], (128, 128)).T
        rows = pl.ds(g * 128, 128)
        cmask[rows, :] = jnp.where(first <= 0.0, one, zero).astype(BF16)
        for k in range(2 * (g // 2) + 2):
            s = lane + 128.0 * k
            keep = s >= first
            if k == g:
                keep = keep & (lane <= sub)
            value = jnp.where(keep, one, zero) if k <= g else zero
            mask[rows, pl.ds(k * 128, 128)] = value.astype(BF16)

    def row(r):
        return dl[pl.ds(r, 1), :]

    def gated(cond, x):
        return jnp.where(cond, x, 0.0)

    first = df[0:1, :]

    def prefix(p, u, c):
        rows = pl.ds(*PARTS[c])
        send_w(p, u, c, wo.at[p - 1, u]).wait_recv()
        wo[p - 1, u, rows] = tails[head_of(p, u), rows] + gated(row(8) == row(7), wr[p - 1, u, rows])
        if p < 3:
            send_w(p + 1, u, c, wo.at[p - 1, u]).start()
        else:
            @pl.when(z != n_z - 1)
            def _():
                send_x(2, u, c, wo.at[2, u]).start()

    def suffix(p, u, c):
        rows = pl.ds(*PARTS[c])
        send_s(p, u, c, so.at[p, u]).wait_recv()
        so[p, u, rows] = gated(row(8) == row(11 - p), tails[head_of(p, u), rows]) + sr[p, u, rows]
        if p:
            send_s(p - 1, u, c, so.at[p, u]).start()
        else:
            send_x(0, u, c, so.at[0, u]).start()

            @pl.when(z != 0)
            def _():
                send_x(6, u, c, so.at[0, u]).start()

    def prefixes(p, u):
        for c in splits:
            prefix(p, u, c)

    def suffixes(p, u):
        for c in splits:
            suffix(p, u, c)

    def both(p, u):
        for c in splits:
            prefix(p, u, c)
            suffix(3 - p, u, c)

    def steps(h):
        v = lax.rem(h, 2)
        first_z, last_z = z == 0, z == n_z - 1
        for p in (1, 2, 3):
            @pl.when(first_z & (h == 2 * p))
            def _():
                prefixes(p, 1)

            @pl.when(last_z & (h == 2 * p))
            def _():
                suffixes(3 - p, 1)

        for p in (1, 2, 3):
            @pl.when((z != 0) & (z != n_z - 1) & (h // 2 == p - 1))
            def _():
                both(p, v)

            @pl.when(first_z & (h // 2 == p - 1))
            def _():
                suffixes(3 - p, v)

            @pl.when(last_z & (h // 2 == p - 1))
            def _():
                prefixes(p, v)

        for p in (1, 2, 3):
            @pl.when(first_z & (h == 2 * p - 1))
            def _():
                prefixes(p, 0)

            @pl.when(last_z & (h == 2 * p - 1))
            def _():
                suffixes(3 - p, 0)

    def handle_4(u):
        for c in splits:
            rows = pl.ds(*PARTS[c])
            send_x(0, u, c, so.at[0, u]).wait_recv()
            send_x(1, u, c, xr.at[0, u]).start()

            @pl.when(z == n_z - 1)
            def _():
                xo[0, u, rows] = wo[2, u, rows] + gated(row(8) == row(4), xr[0, u, rows])
                send_x(2, u, c, xo.at[0, u]).start()
                send_x(7, u, c, xo.at[0, u]).start()

    def handle_5(u, here):
        for c in splits:
            rows = pl.ds(*PARTS[c])
            send_x(2, u, c, xo.at[0, u]).wait_recv()
            carried = gated(first == row(7), xr[2, u, rows])
            if not here:
                send_x(6, u, c, so.at[0, u]).wait_recv()
                carried = carried + gated(first == row(3), xr[6, u, rows])
            car[0, u, rows] = carried
            if not here:
                xo[1, u, rows] = tails[head_of(0, u), rows] + gated(row(8) == first, carried)
                send_x(3, u, c, xo.at[1, u]).start()

    head_rows = pl.ds(0, SENT)

    def last_3(u):
        for c in splits:
            send_x(4, u, c, so.at[0, u]).wait_recv()
        car[3, u, head_rows] = (
            gated(first == row(7), wr[2, u, head_rows])
            + gated(first == row(4), xr[0, u, head_rows])
            + gated(first == row(0), xr[4, u, head_rows])
        )

    def last_2(u):
        for c in splits:
            send_x(1, u, c, so.at[0, u]).wait_recv()
            send_x(5, u, c, so.at[0, u]).wait_recv()
        car[2, u, head_rows] = (
            gated(first == row(7), wr[1, u, head_rows])
            + gated(first == row(5), xr[1, u, head_rows])
            + gated(first == row(1), xr[5, u, head_rows])
        )

    def last_1(u):
        @pl.when(z == 1)
        def _():
            for c in splits:
                send_x(7, u, c, so.at[0, u]).wait_recv()
            car[1, u] = gated(first == row(7), wr[0, u]) + gated(first == row(6), xr[7, u])

        @pl.when(z != 1)
        def _():
            for c in splits:
                send_x(3, u, c, so.at[0, u]).wait_recv()
            car[1, u] = gated(first == row(7), xr[3, u])

    @pl.loop(0, heads)
    def _(h):
        steps(h)
        v = lax.rem(h, 2)
        for slot, kind, stage in SLOTS:
            @pl.when((h == slot) & (z == 0))
            def _():
                for u in range(2):
                    suffix_over(stage, kind, u, True)

            if stage == 0:
                @pl.when((h == slot + kind) & (z != 0))
                def _():
                    for u in range(2):
                        suffix_over(stage, kind, u, False)

        @pl.when((h // 2 == 3) & ((z == 0) | (z == n_z - 1)))
        def _():
            handle_4(v)

        @pl.when((h // 2 == 3) & (z != 0))
        def _():
            handle_5(v, False)

        @pl.when((h // 2 == 3) & (z != 0) & (z != n_z - 1))
        def _():
            handle_4(v)

        load(0, h).wait()
        qf[h] = feature_map(qraw[h])
        blk = 256
        for b in range(tok // blk):
            rows = pl.ds(b * blk, blk)
            width = (b + 1) * blk
            scores = jnp.dot(qf[h, rows, :], kft[h, :, pl.ds(0, width)], preferred_element_type=F32)
            weights = scores.astype(BF16) * mask[rows, pl.ds(0, width)]
            values = jnp.concatenate([vraw[h, pl.ds(0, width), :], ones_v[:width]], axis=1)
            nd[h, rows, :] = jnp.dot(weights, values, preferred_element_type=F32)

    sqacc[...] = jnp.zeros_like(sqacc)

    def finish(p, u):
        h = head_of(p, u)
        carried = car[p, u]
        norm = jnp.broadcast_to(carried[128:129, :], (128, 128)).T
        both = jnp.concatenate([carried[:128, :], norm], axis=1)
        high = both.astype(BF16)
        low = (both - high.astype(F32)).astype(BF16)
        right = jnp.concatenate([high, low], axis=0)

        for b in range(tok // 256):
            rows = pl.ds(b * 256, 256)
            q = qf[h, rows, :] * cmask[rows, :]
            extra = jnp.dot(jnp.concatenate([q, q], axis=1), right, preferred_element_type=F32)
            total = nd[h, rows, :] + extra
            result = total[:, :128] / total[:, 128:]
            att[h, rows, :] = result
            sqacc[rows, :] += result * result

    def late(u):
        @pl.when(z == 0)
        def _():
            handle_5(u, True)

    last_3(0)
    finish(3, 0)
    late(0)
    last_3(1)
    finish(3, 1)
    late(1)
    finish(0, 0)
    finish(0, 1)
    last_2(0)
    finish(2, 0)
    last_1(0)
    finish(1, 0)
    last_2(1)
    finish(2, 1)
    last_1(1)
    finish(1, 1)

    for g in range(groups):
        sq[0, pl.ds(g, 1), :] = jnp.sum(sqacc[pl.ds(g * 128, 128), :].T, axis=0, keepdims=True)

    def send_sq(j):
        return send(sq.at[0], sq.at[j], sq_s.at[j - 1], sq_r.at[j - 1], peer(j))

    for j in range(1, n_head):
        send_sq(j).start()
    for j in range(1, n_head):
        send_sq(j).wait_recv()
    total = jnp.sum(sq[...], axis=0)
    scale = lax.rsqrt(total / n_feat + 1e-06)
    gains.wait()

    for g in range(groups):
        rows = pl.ds(g * 128, 128)
        factor = jnp.broadcast_to(scale[g : g + 1, :], (128, 128)).T
        for h in range(heads):
            cols = pl.ds(h * E, E)
            weight = gain[cols].astype(F32)[None, :]
            out[rows, cols] = (att[h, rows, :] * factor * weight).astype(BF16)

    for j in range(1, n_head):
        send_sq(j).wait_send()
    @pl.when(wrapped)
    def _():
        for u in range(heads // 4):
            for c in splits:
                for stage in (0, 1):
                    for kind in (0, 1):
                        send_relay(stage, kind, u, c, xo.at[0, u]).wait_send()

    for u in range(heads // 4):
        for c in splits:
            for p in (1, 2, 3):
                send_w(p, u, c, wo.at[0, u]).wait_send()
            for p in (0, 1, 2):
                send_s(p, u, c, so.at[0, u]).wait_send()
            for kind in (0, 1, 2, 4, 5):
                send_x(kind, u, c, xo.at[0, u]).wait_send()

            @pl.when(z != 0)
            def _():
                send_x(3, u, c, xo.at[0, u]).wait_send()
                send_x(6, u, c, xo.at[0, u]).wait_send()

            @pl.when(z == n_z - 1)
            def _():
                send_x(7, u, c, xo.at[0, u]).wait_send()


def body(n_seq, n_head, query_act, key_act, value_act, norm_gain, doc_lengths):
    tok, width = query_act.shape
    heads = width // E
    two = heads // 4
    any_spec = pl.BlockSpec(memory_space=pl.ANY)
    dma = pltpu.SemaphoreType.DMA
    state = lambda n: pltpu.VMEM((n, two, ROWS, 128), F32)
    arrivals = lambda n: dma((n, two, len(PARTS)))
    return pl.pallas_call(
        functools.partial(kernel, n_seq, n_head, n_head * width),
        out_shape=pltpu.VMEM((tok, width), BF16),
        in_specs=[any_spec] * 5,
        out_specs=pl.BlockSpec(memory_space=pltpu.VMEM),
        scratch_shapes=[
            pltpu.VMEM((heads, tok, E), BF16),
            pltpu.VMEM((heads, tok, E), BF16),
            pltpu.VMEM((heads, tok, E), BF16),
            pltpu.VMEM((heads, tok, E), BF16),
            pltpu.VMEM((heads, E, tok), BF16),
            pltpu.VMEM((heads, ROWS, 128), F32),
            pltpu.VMEM((heads, tok, 256), F32),
            pltpu.VMEM((heads, tok, E), F32),
            pltpu.VMEM((tok, 128), F32),
            pltpu.VMEM((tok, tok), BF16),
            pltpu.VMEM((tok, 128), BF16),
            pltpu.VMEM((128, tok), BF16),
            pltpu.VMEM((16, 128), jnp.int32),
            pltpu.VMEM((8, 128), jnp.int32),
            pltpu.SMEM(doc_lengths.shape, jnp.int32),
            pltpu.VMEM((width,), BF16),
            state(3), state(3), state(8),
            state(3), state(3), state(2), state(4),
            pltpu.VMEM((n_head, 8, 128), F32),
            dma((3, heads)), dma((2,)),
            pltpu.VMEM((2, 2, two, ROWS, 128), F32),
            dma((2, 2, two, len(PARTS))), dma((2, 2, two, len(PARTS))),
            arrivals(3), arrivals(3), arrivals(3), arrivals(3),
            arrivals(8), arrivals(8),
            dma((n_head - 1,)), dma((n_head - 1,)),
        ],
        compiler_params=pltpu.CompilerParams(
            collective_id=1, has_side_effects=True, vmem_limit_bytes=56 * 1024 * 1024
        ),
        name="attend",
    )(query_act, key_act, value_act, norm_gain, doc_lengths)


def solution(mesh):
    in_specs = (P("seq", "head"), P("seq", "head"), P("seq", "head"), P("head"), P())
    fn = functools.partial(body, mesh.shape["seq"], mesh.shape["head"])
    return jax.shard_map(fn, mesh=mesh, in_specs=in_specs, out_specs=P("seq", "head"), check_vma=False)
```

```python
import functools

import jax
import jax.numpy as jnp
from jax import lax
from jax.experimental import pallas as pl
from jax.experimental.pallas import tpu as pltpu
from jax.sharding import PartitionSpec as P

E = 128
ROWS = 136
PARTS = ((0, 129),)
SENT = 129
DIRECT = (1,)
SLOTS = ((3, 0, 1), (6, 0, 2))
MESH = pl.DeviceIdType.MESH
F32 = jnp.float32
BF16 = jnp.bfloat16


def feature_map(x):
    x = x.astype(F32)
    return jnp.where(x > 0.0, x + 1.0, jnp.exp(x)).astype(BF16)


def kernel(
    n_seq, n_head, n_feat,
    q_hbm, k_hbm, v_hbm, gain_hbm, len_hbm,
    out,
    qraw, kraw, vraw, qf, kft, tails, nd, att, sqacc,
    mask, cmask, tmask, dl, df,
    len_ref, gain, wr, sr, xr, wo, so, xo, car, sq,
    in_sem, small_sem,
    rl, rl_s, rl_r, wr_s, wr_r, sr_s, sr_r, xr_s, xr_r, sq_s, sq_r,
):
    heads, tok, _ = qraw.shape
    groups = tok // 128
    i = lax.axis_index("seq")
    hd = lax.axis_index("head")

    n_z = 8
    z = lax.rem(i, n_z)
    wrapped = z == 0
    over, back = 'over', 'back'

    near = {d: lax.rem(i + d + n_seq, n_seq) for d in (-8, -7, -2, -1, 1, 2, 7, 8)}
    near[over] = jnp.where(wrapped, near[-8], near[8])
    near[back] = jnp.where(wrapped, near[8], near[-8])
    classes = [lax.rem(i - p + 4 * n_seq, 4) for p in range(4)]

    def shard(d):
        return (near[d], hd)

    others = [lax.rem(hd + j, n_head) for j in range(n_head)]

    def peer(j):
        return (i, others[j])

    def odd(j):
        return jnp.where((j == 1) | (j == 3) | (j == 5) | (j == 7), 1, 0)

    def position(j):
        return jnp.where(j < 4, 3 * odd(j), 1 + odd(j))

    def second(j):
        return jnp.where((j == 2) | (j == 3) | (j >= 6), 1, 0)

    def head_of(p, u):
        if isinstance(p, int):
            return classes[p] + 4 * u
        own = jnp.where(p == 0, classes[0], jnp.where(p == 1, classes[1], jnp.where(p == 2, classes[2], classes[3])))
        return own + 4 * u

    def col(ref, h):
        return ref.at[:, pl.ds(pl.multiple_of(h * E, E), E)]

    def load(which, h):
        src, dst = ((q_hbm, qraw), (k_hbm, kraw), (v_hbm, vraw))[which]
        return pltpu.make_async_copy(col(src, h), dst.at[h], in_sem.at[which, h])

    lengths = pltpu.make_async_copy(len_hbm, len_ref, small_sem.at[0])
    gains = pltpu.make_async_copy(gain_hbm, gain, small_sem.at[1])
    lengths.start()
    barrier = pltpu.get_barrier_semaphore()
    senders = [shard(d) for d in (-1, 1, back, -7)]
    senders += [peer(j) for j in range(1, n_head)]
    for dev in senders:
        pl.semaphore_signal(barrier, inc=1, device_id=dev, device_id_type=MESH)

    for cond, d in ((z == 0, -8), (z == 1, -2)):
        @pl.when(cond)
        def _():
            pl.semaphore_signal(barrier, inc=1, device_id=shard(d), device_id_type=MESH)

    @pl.loop(0, heads)
    def _(j):
        h = head_of(position(j), second(j))
        load(1, h).start()
        load(2, h).start()

    @pl.loop(0, heads)
    def _(h):
        load(0, h).start()

    gains.start()
    lengths.wait()

    base = i * tok
    lane8 = lax.broadcasted_iota(jnp.int32, (8, 128), 1)
    sub8 = lax.broadcasted_iota(jnp.int32, (8, 128), 0)
    sub16 = lax.broadcasted_iota(jnp.int32, (16, 128), 0)
    pos_tok = base + sub8 * 128 + lane8
    pos_last = (i - 7 + sub16) * tok - 1
    pos_first = jnp.zeros((8, 128), jnp.int32) + base
    st_tok = jnp.zeros((8, 128), jnp.int32)
    st_last = jnp.where(pos_last < 0, -1, 0)
    st_first = jnp.zeros((8, 128), jnp.int32)
    end = jnp.int32(0)
    for d in range(len_ref.shape[0]):
        end = end + len_ref[d]
        st_tok = jnp.where(pos_tok >= end, end, st_tok)
        st_last = jnp.where(pos_last >= end, end, st_last)
        st_first = jnp.where(pos_first >= end, end, st_first)
    dl[...] = st_last
    df[...] = st_first

    lane = lax.broadcasted_iota(jnp.int32, (128, 128), 1).astype(F32)
    sub = lax.broadcasted_iota(jnp.int32, (128, 128), 0).astype(F32)
    st_loc = (st_tok - base).astype(F32)
    tail_start = (st_last[8:9, :] - base).astype(F32)
    one, zero = jnp.ones((128, 128), F32), jnp.zeros((128, 128), F32)
    for g in range(groups):
        rows = pl.ds(g * 128, 128)
        tmask[:, rows] = jnp.where(lane + 128.0 * g >= tail_start, one, zero).astype(BF16)

    pl.semaphore_wait(barrier, len(senders) + jnp.where((z == 0) | (z == n_z - 1), 1, 0))

    ones_v = jnp.ones((tok, 128), BF16)

    def send(src, dst, s_sem, r_sem, dev):
        return pltpu.make_async_remote_copy(
            src_ref=src, dst_ref=dst, send_sem=s_sem, recv_sem=r_sem, device_id=dev, device_id_type=MESH
        )

    def part(ref, c):
        return ref.at[pl.ds(*PARTS[c]), :]

    def send_w(p, u, c, src):
        w = (p - 1, u, c)
        return send(part(src, c), part(wr.at[p - 1, u], c), wr_s.at[w], wr_r.at[w], shard(1))

    def send_s(p, u, c, src):
        w = (p, u, c)
        return send(part(src, c), part(sr.at[p, u], c), sr_s.at[w], sr_r.at[w], shard(-1))

    def send_x(kind, u, c, src):
        dist = (7, -1, 1, 1, over, 8, 8, 2)[kind]
        w = (kind, u, c)
        return send(part(src, c), part(xr.at[kind, u], c), xr_s.at[w], xr_r.at[w], shard(dist))

    splits = range(len(PARTS))

    def send_relay(stage, kind, u, c, src):
        w = (stage, kind, u, c)
        return send(part(src, c), part(rl.at[stage, kind, u], c), rl_s.at[w], rl_r.at[w], shard(over))

    def suffix_on(kind, u, c, source):
        if kind in DIRECT:
            send_x(4 + kind, u, c, source).start()
            return

        @pl.when(z != 0)
        def _():
            send_x(4 + kind, u, c, source).start()

        @pl.when(z == 0)
        def _():
            send_relay(0, kind, u, c, source).start()

    def relay(stage, kind, u):
        for c in splits:
            send_relay(stage - 1, kind, u, c, so.at[2, u]).wait_recv()
            src = rl.at[stage - 1, kind, u]
            (send_relay(1, kind, u, c, src) if stage == 1 else send_x(4 + kind, u, c, src)).start()

    @pl.loop(0, heads)
    def _(j):
        p = position(j)
        u = second(j)
        h = head_of(p, u)
        load(1, h).wait()
        kt = feature_map(kraw[h]).T
        kft[h] = kt
        load(2, h).wait()
        state = jnp.dot(
            kt * tmask[...],
            jnp.concatenate([vraw[h], ones_v], axis=1),
            preferred_element_type=F32,
        )
        tails[h, pl.ds(0, 128), :] = state[:, :128]
        tails[h, pl.ds(128, 8), :] = state[:, 128:].T[0:8, :]

        @pl.when((j < 4) & (p == 0))
        def _():
            for c in splits:
                send_w(1, u, c, tails.at[h]).start()

        @pl.when((j < 4) & (p == 3))
        def _():
            for c in splits:
                send_s(2, u, c, tails.at[h]).start()
                suffix_on(0, u, c, tails.at[h])

    for g in range(groups):
        first = jnp.broadcast_to(st_loc[g : g + 1, :], (128, 128)).T
        rows = pl.ds(g * 128, 128)
        cmask[rows, :] = jnp.where(first <= 0.0, one, zero).astype(BF16)
        for k in range(2 * (g // 2) + 2):
            s = lane + 128.0 * k
            keep = s >= first
            if k == g:
                keep = keep & (lane <= sub)
            value = jnp.where(keep, one, zero) if k <= g else zero
            mask[rows, pl.ds(k * 128, 128)] = value.astype(BF16)

    def row(r):
        return dl[pl.ds(r, 1), :]

    def gated(cond, x):
        return jnp.where(cond, x, 0.0)

    first = df[0:1, :]

    def prefix(p, u, c):
        rows = pl.ds(*PARTS[c])
        send_w(p, u, c, wo.at[p - 1, u]).wait_recv()
        wo[p - 1, u, rows] = tails[head_of(p, u), rows] + gated(row(8) == row(7), wr[p - 1, u, rows])
        if p < 3:
            send_w(p + 1, u, c, wo.at[p - 1, u]).start()
        else:
            @pl.when(z != n_z - 1)
            def _():
                send_x(2, u, c, wo.at[2, u]).start()

    def suffix(p, u, c):
        rows = pl.ds(*PARTS[c])
        send_s(p, u, c, so.at[p, u]).wait_recv()
        so[p, u, rows] = gated(row(8) == row(11 - p), tails[head_of(p, u), rows]) + sr[p, u, rows]
        if p:
            send_s(p - 1, u, c, so.at[p, u]).start()
            if p == 2:
                suffix_on(1, u, c, so.at[2, u])
        else:
            send_x(0, u, c, so.at[0, u]).start()

            @pl.when(z != 0)
            def _():
                send_x(6, u, c, so.at[0, u]).start()

    def prefixes(p, u):
        for c in splits:
            prefix(p, u, c)

    def suffixes(p, u):
        for c in splits:
            suffix(p, u, c)

    def both(p, u):
        for c in splits:
            prefix(p, u, c)
            suffix(3 - p, u, c)

    def steps(h):
        v = odd(h)
        first_z, last_z = z == 0, z == n_z - 1
        for p in (1, 2, 3):
            @pl.when(first_z & (h == 2 * p))
            def _():
                prefixes(p, 1)

            @pl.when(last_z & (h == 2 * p))
            def _():
                suffixes(3 - p, 1)

        for p in (1, 2, 3):
            @pl.when((z != 0) & (z != n_z - 1) & (h >= 2 * p - 2) & (h < 2 * p))
            def _():
                both(p, v)

            @pl.when(first_z & (h >= 2 * p - 2) & (h < 2 * p))
            def _():
                suffixes(3 - p, v)

            @pl.when(last_z & (h >= 2 * p - 2) & (h < 2 * p))
            def _():
                prefixes(p, v)

        for p in (1, 2, 3):
            @pl.when(first_z & (h == 2 * p - 1))
            def _():
                prefixes(p, 0)

            @pl.when(last_z & (h == 2 * p - 1))
            def _():
                suffixes(3 - p, 0)

    def handle_4(u):
        for c in splits:
            rows = pl.ds(*PARTS[c])
            send_x(0, u, c, so.at[0, u]).wait_recv()
            send_x(1, u, c, xr.at[0, u]).start()

            @pl.when(z == n_z - 1)
            def _():
                xo[0, u, rows] = wo[2, u, rows] + gated(row(8) == row(4), xr[0, u, rows])
                send_x(2, u, c, xo.at[0, u]).start()
                send_x(7, u, c, xo.at[0, u]).start()

    def handle_5(u, here):
        for c in splits:
            rows = pl.ds(*PARTS[c])
            send_x(2, u, c, xo.at[0, u]).wait_recv()
            carried = gated(first == row(7), xr[2, u, rows])
            if not here:
                send_x(6, u, c, so.at[0, u]).wait_recv()
                carried = carried + gated(first == row(3), xr[6, u, rows])
            car[0, u, rows] = carried
            if not here:
                xo[1, u, rows] = tails[head_of(0, u), rows] + gated(row(8) == first, carried)
                send_x(3, u, c, xo.at[1, u]).start()

    head_rows = pl.ds(0, SENT)

    def last_3(u):
        for c in splits:
            send_x(4, u, c, so.at[0, u]).wait_recv()
        car[3, u, head_rows] = (
            gated(first == row(7), wr[2, u, head_rows])
            + gated(first == row(4), xr[0, u, head_rows])
            + gated(first == row(0), xr[4, u, head_rows])
        )

    def last_2(u):
        for c in splits:
            send_x(1, u, c, so.at[0, u]).wait_recv()
            send_x(5, u, c, so.at[0, u]).wait_recv()
        car[2, u, head_rows] = (
            gated(first == row(7), wr[1, u, head_rows])
            + gated(first == row(5), xr[1, u, head_rows])
            + gated(first == row(1), xr[5, u, head_rows])
        )

    def last_1(u):
        @pl.when(z == 1)
        def _():
            for c in splits:
                send_x(7, u, c, so.at[0, u]).wait_recv()
            car[1, u] = gated(first == row(7), wr[0, u]) + gated(first == row(6), xr[7, u])

        @pl.when(z != 1)
        def _():
            for c in splits:
                send_x(3, u, c, so.at[0, u]).wait_recv()
            car[1, u] = gated(first == row(7), xr[3, u])

    @pl.loop(0, heads)
    def _(h):
        steps(h)
        v = odd(h)
        for slot, kind, stage in SLOTS:
            @pl.when((h == slot) & (z == 0))
            def _():
                for u in range(2):
                    relay(stage, kind, u)

        @pl.when((h >= 6) & ((z == 0) | (z == n_z - 1)))
        def _():
            handle_4(v)

        @pl.when((h >= 6) & (z != 0))
        def _():
            handle_5(v, False)

        @pl.when((h >= 6) & (z != 0) & (z != n_z - 1))
        def _():
            handle_4(v)

        load(0, h).wait()
        qf[h] = feature_map(qraw[h])
        blk = 256
        for b in range(tok // blk):
            rows = pl.ds(b * blk, blk)
            width = (b + 1) * blk
            scores = jnp.dot(qf[h, rows, :], kft[h, :, pl.ds(0, width)], preferred_element_type=F32)
            weights = scores.astype(BF16) * mask[rows, pl.ds(0, width)]
            values = jnp.concatenate([vraw[h, pl.ds(0, width), :], ones_v[:width]], axis=1)
            nd[h, rows, :] = jnp.dot(weights, values, preferred_element_type=F32)

    sqacc[...] = jnp.zeros_like(sqacc)

    def finish(p, u):
        h = head_of(p, u)
        carried = car[p, u]
        norm = jnp.broadcast_to(carried[128:129, :], (128, 128)).T
        both = jnp.concatenate([carried[:128, :], norm], axis=1)
        high = both.astype(BF16)
        low = (both - high.astype(F32)).astype(BF16)
        right = jnp.concatenate([high, low], axis=0)

        for b in range(tok // 256):
            rows = pl.ds(b * 256, 256)
            q = qf[h, rows, :] * cmask[rows, :]
            extra = jnp.dot(jnp.concatenate([q, q], axis=1), right, preferred_element_type=F32)
            total = nd[h, rows, :] + extra
            result = total[:, :128] / total[:, 128:]
            att[h, rows, :] = result
            sqacc[rows, :] += result * result

    def late(u):
        @pl.when(z == 0)
        def _():
            handle_5(u, True)

    last_3(0)
    finish(3, 0)
    late(0)
    last_3(1)
    finish(3, 1)
    late(1)
    finish(0, 0)
    finish(0, 1)
    last_2(0)
    finish(2, 0)
    last_1(0)
    finish(1, 0)
    last_2(1)
    finish(2, 1)
    last_1(1)
    finish(1, 1)

    for g in range(groups):
        sq[0, pl.ds(g, 1), :] = jnp.sum(sqacc[pl.ds(g * 128, 128), :].T, axis=0, keepdims=True)

    def send_sq(j):
        return send(sq.at[0], sq.at[j], sq_s.at[j - 1], sq_r.at[j - 1], peer(j))

    for j in range(1, n_head):
        send_sq(j).start()
    for j in range(1, n_head):
        send_sq(j).wait_recv()
    total = jnp.sum(sq[...], axis=0)
    scale = lax.rsqrt(total / n_feat + 1e-06)
    gains.wait()

    for g in range(groups):
        rows = pl.ds(g * 128, 128)
        factor = jnp.broadcast_to(scale[g : g + 1, :], (128, 128)).T
        for h in range(heads):
            cols = pl.ds(h * E, E)
            weight = gain[cols].astype(F32)[None, :]
            out[rows, cols] = (att[h, rows, :] * factor * weight).astype(BF16)

    for j in range(1, n_head):
        send_sq(j).wait_send()
    @pl.when(wrapped)
    def _():
        for u in range(heads // 4):
            for c in splits:
                for stage in (0, 1):
                    for kind in (0,):
                        send_relay(stage, kind, u, c, xo.at[0, u]).wait_send()

    for u in range(heads // 4):
        for c in splits:
            for p in (1, 2, 3):
                send_w(p, u, c, wo.at[0, u]).wait_send()
            for p in (0, 1, 2):
                send_s(p, u, c, so.at[0, u]).wait_send()
            for kind in (0, 1, 2, 4, 5):
                send_x(kind, u, c, xo.at[0, u]).wait_send()

            @pl.when(z != 0)
            def _():
                send_x(3, u, c, xo.at[0, u]).wait_send()
                send_x(6, u, c, xo.at[0, u]).wait_send()

            @pl.when(z == n_z - 1)
            def _():
                send_x(7, u, c, xo.at[0, u]).wait_send()


def body(n_seq, n_head, query_act, key_act, value_act, norm_gain, doc_lengths):
    tok, width = query_act.shape
    heads = width // E
    two = heads // 4
    any_spec = pl.BlockSpec(memory_space=pl.ANY)
    dma = pltpu.SemaphoreType.DMA
    state = lambda n: pltpu.VMEM((n, two, ROWS, 128), F32)
    arrivals = lambda n: dma((n, two, len(PARTS)))
    return pl.pallas_call(
        functools.partial(kernel, n_seq, n_head, n_head * width),
        out_shape=pltpu.VMEM((tok, width), BF16),
        in_specs=[any_spec] * 5,
        out_specs=pl.BlockSpec(memory_space=pltpu.VMEM),
        scratch_shapes=[
            pltpu.VMEM((heads, tok, E), BF16),
            pltpu.VMEM((heads, tok, E), BF16),
            pltpu.VMEM((heads, tok, E), BF16),
            pltpu.VMEM((heads, tok, E), BF16),
            pltpu.VMEM((heads, E, tok), BF16),
            pltpu.VMEM((heads, ROWS, 128), F32),
            pltpu.VMEM((heads, tok, 256), F32),
            pltpu.VMEM((heads, tok, E), F32),
            pltpu.VMEM((tok, 128), F32),
            pltpu.VMEM((tok, tok), BF16),
            pltpu.VMEM((tok, 128), BF16),
            pltpu.VMEM((128, tok), BF16),
            pltpu.VMEM((16, 128), jnp.int32),
            pltpu.VMEM((8, 128), jnp.int32),
            pltpu.SMEM(doc_lengths.shape, jnp.int32),
            pltpu.VMEM((width,), BF16),
            state(3), state(3), state(8),
            state(3), state(3), state(2), state(4),
            pltpu.VMEM((n_head, 8, 128), F32),
            dma((3, heads)), dma((2,)),
            pltpu.VMEM((2, 2, two, ROWS, 128), F32),
            dma((2, 2, two, len(PARTS))), dma((2, 2, two, len(PARTS))),
            arrivals(3), arrivals(3), arrivals(3), arrivals(3),
            arrivals(8), arrivals(8),
            dma((n_head - 1,)), dma((n_head - 1,)),
        ],
        compiler_params=pltpu.CompilerParams(
            collective_id=1, has_side_effects=True, vmem_limit_bytes=56 * 1024 * 1024
        ),
        name="attend",
    )(query_act, key_act, value_act, norm_gain, doc_lengths)


def solution(mesh):
    in_specs = (P("seq", "head"), P("seq", "head"), P("seq", "head"), P("head"), P())
    fn = functools.partial(body, mesh.shape["seq"], mesh.shape["head"])
    return jax.shard_map(fn, mesh=mesh, in_specs=in_specs, out_specs=P("seq", "head"), check_vma=False)
```

```python
import functools

import jax
import jax.numpy as jnp
from jax import lax
from jax.experimental import pallas as pl
from jax.experimental.pallas import tpu as pltpu
from jax.sharding import PartitionSpec as P

E = 128
ROWS = 136
PARTS = ((0, 129),)
SENT = 129
DIRECT = (1,)
SLOTS = ((3, 0, 1), (6, 0, 2))
MESH = pl.DeviceIdType.MESH
F32 = jnp.float32
BF16 = jnp.bfloat16


def feature_map(x):
    x = x.astype(F32)
    return jnp.where(x > 0.0, x + 1.0, jnp.exp(x)).astype(BF16)


def kernel(
    n_seq, n_head, n_feat,
    q_hbm, k_hbm, v_hbm, gain_hbm, len_hbm,
    out,
    qraw, kraw, vraw, qf, kft, tails, nd, att, sqacc,
    mask, cmask, tmask, dl, df,
    len_ref, gain, wr, sr, xr, wo, so, xo, car, sq,
    in_sem, small_sem,
    rl, rl_s, rl_r, wr_s, wr_r, sr_s, sr_r, xr_s, xr_r, sq_s, sq_r,
):
    heads, tok, _ = qraw.shape
    groups = tok // 128
    i = lax.axis_index("seq")
    hd = lax.axis_index("head")

    n_z = 8
    z = lax.rem(i, n_z)
    wrapped = z == 0
    over, back = 'over', 'back'

    near = {d: lax.rem(i + d + n_seq, n_seq) for d in (-8, -7, -2, -1, 1, 2, 7, 8)}
    near[over] = jnp.where(wrapped, near[-8], near[8])
    near[back] = jnp.where(wrapped, near[8], near[-8])
    classes = [lax.rem(i - p + 4 * n_seq, 4) for p in range(4)]

    def shard(d):
        return (near[d], hd)

    others = [lax.rem(hd + j, n_head) for j in range(n_head)]

    def peer(j):
        return (i, others[j])

    def odd(j):
        return jnp.where((j == 1) | (j == 3) | (j == 5) | (j == 7), 1, 0)

    def position(j):
        return jnp.where(j < 4, 3 * odd(j), 1 + odd(j))

    def second(j):
        return jnp.where((j == 2) | (j == 3) | (j >= 6), 1, 0)

    def head_of(p, u):
        if isinstance(p, int):
            return classes[p] + 4 * u
        own = jnp.where(p == 0, classes[0], jnp.where(p == 1, classes[1], jnp.where(p == 2, classes[2], classes[3])))
        return own + 4 * u

    def col(ref, h):
        return ref.at[:, pl.ds(pl.multiple_of(h * E, E), E)]

    def load(which, h):
        src, dst = ((q_hbm, qraw), (k_hbm, kraw), (v_hbm, vraw))[which]
        return pltpu.make_async_copy(col(src, h), dst.at[h], in_sem.at[which, h])

    lengths = pltpu.make_async_copy(len_hbm, len_ref, small_sem.at[0])
    gains = pltpu.make_async_copy(gain_hbm, gain, small_sem.at[1])
    lengths.start()
    barrier = pltpu.get_barrier_semaphore()
    senders = [shard(d) for d in (-1, 1, back, -7)]
    senders += [peer(j) for j in range(1, n_head)]
    for dev in senders:
        pl.semaphore_signal(barrier, inc=1, device_id=dev, device_id_type=MESH)

    for cond, d in ((z == 0, -8), (z == 1, -2)):
        @pl.when(cond)
        def _():
            pl.semaphore_signal(barrier, inc=1, device_id=shard(d), device_id_type=MESH)

    @pl.loop(0, heads)
    def _(j):
        h = head_of(position(j), second(j))
        load(1, h).start()
        load(2, h).start()

    @pl.loop(0, heads)
    def _(h):
        load(0, h).start()

    gains.start()
    lengths.wait()

    base = i * tok
    lane8 = lax.broadcasted_iota(jnp.int32, (8, 128), 1)
    sub8 = lax.broadcasted_iota(jnp.int32, (8, 128), 0)
    sub16 = lax.broadcasted_iota(jnp.int32, (16, 128), 0)
    pos_tok = base + sub8 * 128 + lane8
    pos_last = (i - 7 + sub16) * tok - 1
    pos_first = jnp.zeros((8, 128), jnp.int32) + base
    st_tok = jnp.zeros((8, 128), jnp.int32)
    st_last = jnp.where(pos_last < 0, -1, 0)
    st_first = jnp.zeros((8, 128), jnp.int32)
    end = jnp.int32(0)
    for d in range(len_ref.shape[0]):
        end = end + len_ref[d]
        st_tok = jnp.where(pos_tok >= end, end, st_tok)
        st_last = jnp.where(pos_last >= end, end, st_last)
        st_first = jnp.where(pos_first >= end, end, st_first)
    dl[...] = st_last
    df[...] = st_first

    lane = lax.broadcasted_iota(jnp.int32, (128, 128), 1).astype(F32)
    sub = lax.broadcasted_iota(jnp.int32, (128, 128), 0).astype(F32)
    st_loc = (st_tok - base).astype(F32)
    tail_start = (st_last[8:9, :] - base).astype(F32)
    one, zero = jnp.ones((128, 128), F32), jnp.zeros((128, 128), F32)
    for g in range(groups):
        rows = pl.ds(g * 128, 128)
        tmask[:, rows] = jnp.where(lane + 128.0 * g >= tail_start, one, zero).astype(BF16)

    pl.semaphore_wait(barrier, len(senders) + jnp.where((z == 0) | (z == n_z - 1), 1, 0))

    ones_v = jnp.ones((tok, 128), BF16)

    def send(src, dst, s_sem, r_sem, dev):
        return pltpu.make_async_remote_copy(
            src_ref=src, dst_ref=dst, send_sem=s_sem, recv_sem=r_sem, device_id=dev, device_id_type=MESH
        )

    def part(ref, c):
        return ref.at[pl.ds(*PARTS[c]), :]

    def send_w(p, u, c, src):
        w = (p - 1, u, c)
        return send(part(src, c), part(wr.at[p - 1, u], c), wr_s.at[w], wr_r.at[w], shard(1))

    def send_s(p, u, c, src):
        w = (p, u, c)
        return send(part(src, c), part(sr.at[p, u], c), sr_s.at[w], sr_r.at[w], shard(-1))

    def send_x(kind, u, c, src):
        dist = (7, -1, 1, 1, over, 8, 8, 2)[kind]
        w = (kind, u, c)
        return send(part(src, c), part(xr.at[kind, u], c), xr_s.at[w], xr_r.at[w], shard(dist))

    splits = range(len(PARTS))

    def send_relay(stage, kind, u, c, src):
        w = (stage, kind, u, c)
        return send(part(src, c), part(rl.at[stage, kind, u], c), rl_s.at[w], rl_r.at[w], shard(over))

    def suffix_on(kind, u, c, source):
        if kind in DIRECT:
            send_x(4 + kind, u, c, source).start()
            return

        @pl.when(z != 0)
        def _():
            send_x(4 + kind, u, c, source).start()

        @pl.when(z == 0)
        def _():
            send_relay(0, kind, u, c, source).start()

    def relay(stage, kind, u):
        for c in splits:
            send_relay(stage - 1, kind, u, c, so.at[2, u]).wait_recv()
            src = rl.at[stage - 1, kind, u]
            (send_relay(1, kind, u, c, src) if stage == 1 else send_x(4 + kind, u, c, src)).start()

    @pl.loop(0, heads)
    def _(j):
        p = position(j)
        u = second(j)
        h = head_of(p, u)
        load(1, h).wait()
        kt = feature_map(kraw[h]).T
        kft[h] = kt
        load(2, h).wait()
        state = jnp.dot(
            kt * tmask[...],
            jnp.concatenate([vraw[h], ones_v], axis=1),
            preferred_element_type=F32,
        )
        tails[h, pl.ds(0, 128), :] = state[:, :128]
        tails[h, pl.ds(128, 8), :] = state[:, 128:].T[0:8, :]

        @pl.when((j < 4) & (p == 0))
        def _():
            for c in splits:
                send_w(1, u, c, tails.at[h]).start()

        @pl.when((j < 4) & (p == 3))
        def _():
            for c in splits:
                send_s(2, u, c, tails.at[h]).start()
                suffix_on(0, u, c, tails.at[h])

    for g in range(groups):
        first = jnp.broadcast_to(st_loc[g : g + 1, :], (128, 128)).T
        rows = pl.ds(g * 128, 128)
        cmask[rows, :] = jnp.where(first <= 0.0, one, zero).astype(BF16)
        for k in range(2 * (g // 2) + 2):
            s = lane + 128.0 * k
            keep = s >= first
            if k == g:
                keep = keep & (lane <= sub)
            value = jnp.where(keep, one, zero) if k <= g else zero
            mask[rows, pl.ds(k * 128, 128)] = value.astype(BF16)

    def row(r):
        return dl[pl.ds(r, 1), :]

    def gated(cond, x):
        return jnp.where(cond, x, 0.0)

    first = df[0:1, :]

    def prefix(p, u, c):
        rows = pl.ds(*PARTS[c])
        send_w(p, u, c, wo.at[p - 1, u]).wait_recv()
        wo[p - 1, u, rows] = tails[head_of(p, u), rows] + gated(row(8) == row(7), wr[p - 1, u, rows])
        if p < 3:
            send_w(p + 1, u, c, wo.at[p - 1, u]).start()
        else:
            @pl.when(z != n_z - 1)
            def _():
                send_x(2, u, c, wo.at[2, u]).start()

    def suffix(p, u, c):
        rows = pl.ds(*PARTS[c])
        send_s(p, u, c, so.at[p, u]).wait_recv()
        so[p, u, rows] = gated(row(8) == row(11 - p), tails[head_of(p, u), rows]) + sr[p, u, rows]
        if p:
            send_s(p - 1, u, c, so.at[p, u]).start()
            if p == 2:
                suffix_on(1, u, c, so.at[2, u])
        else:
            send_x(0, u, c, so.at[0, u]).start()

            @pl.when(z != 0)
            def _():
                send_x(6, u, c, so.at[0, u]).start()

    def prefixes(p, u):
        for c in splits:
            prefix(p, u, c)

    def suffixes(p, u):
        for c in splits:
            suffix(p, u, c)

    def both(p, u):
        for c in splits:
            prefix(p, u, c)
            suffix(3 - p, u, c)

    def steps(h):
        v = odd(h)
        first_z, last_z = z == 0, z == n_z - 1
        for p in (1, 2, 3):
            @pl.when(first_z & (h == 2 * p))
            def _():
                prefixes(p, 1)

            @pl.when(last_z & (h == 2 * p))
            def _():
                suffixes(3 - p, 1)

        for p in (1, 2, 3):
            @pl.when((z != 0) & (z != n_z - 1) & (h >= 2 * p - 2) & (h < 2 * p))
            def _():
                both(p, v)

            @pl.when(first_z & (h >= 2 * p - 2) & (h < 2 * p))
            def _():
                suffixes(3 - p, v)

            @pl.when(last_z & (h >= 2 * p - 2) & (h < 2 * p))
            def _():
                prefixes(p, v)

        for p in (1, 2, 3):
            @pl.when(first_z & (h == 2 * p - 1))
            def _():
                prefixes(p, 0)

            @pl.when(last_z & (h == 2 * p - 1))
            def _():
                suffixes(3 - p, 0)

    def handle_4(u):
        for c in splits:
            rows = pl.ds(*PARTS[c])
            send_x(0, u, c, so.at[0, u]).wait_recv()
            send_x(1, u, c, xr.at[0, u]).start()

            @pl.when(z == n_z - 1)
            def _():
                xo[0, u, rows] = wo[2, u, rows] + gated(row(8) == row(4), xr[0, u, rows])
                send_x(2, u, c, xo.at[0, u]).start()
                send_x(7, u, c, xo.at[0, u]).start()

    def handle_5(u, here):
        for c in splits:
            rows = pl.ds(*PARTS[c])
            send_x(2, u, c, xo.at[0, u]).wait_recv()
            carried = gated(first == row(7), xr[2, u, rows])
            if not here:
                send_x(6, u, c, so.at[0, u]).wait_recv()
                carried = carried + gated(first == row(3), xr[6, u, rows])
            car[0, u, rows] = carried
            if not here:
                xo[1, u, rows] = tails[head_of(0, u), rows] + gated(row(8) == first, carried)
                send_x(3, u, c, xo.at[1, u]).start()

    head_rows = pl.ds(0, SENT)

    def last_3(u):
        for c in splits:
            send_x(4, u, c, so.at[0, u]).wait_recv()
        car[3, u, head_rows] = (
            gated(first == row(7), wr[2, u, head_rows])
            + gated(first == row(4), xr[0, u, head_rows])
            + gated(first == row(0), xr[4, u, head_rows])
        )

    def last_2(u):
        for c in splits:
            send_x(1, u, c, so.at[0, u]).wait_recv()
            send_x(5, u, c, so.at[0, u]).wait_recv()
        car[2, u, head_rows] = (
            gated(first == row(7), wr[1, u, head_rows])
            + gated(first == row(5), xr[1, u, head_rows])
            + gated(first == row(1), xr[5, u, head_rows])
        )

    def last_1(u):
        @pl.when(z == 1)
        def _():
            for c in splits:
                send_x(7, u, c, so.at[0, u]).wait_recv()
            car[1, u] = gated(first == row(7), wr[0, u]) + gated(first == row(6), xr[7, u])

        @pl.when(z != 1)
        def _():
            for c in splits:
                send_x(3, u, c, so.at[0, u]).wait_recv()
            car[1, u] = gated(first == row(7), xr[3, u])

    @pl.loop(0, heads)
    def _(h):
        steps(h)
        v = odd(h)
        for slot, kind, stage in SLOTS:
            @pl.when((h == slot) & (z == 0))
            def _():
                for u in range(2):
                    relay(stage, kind, u)

        @pl.when((h >= 6) & ((z == 0) | (z == n_z - 1)))
        def _():
            handle_4(v)

        @pl.when((h >= 6) & (z != 0))
        def _():
            handle_5(v, False)

        @pl.when((h >= 6) & (z != 0) & (z != n_z - 1))
        def _():
            handle_4(v)

        load(0, h).wait()
        qf[h] = feature_map(qraw[h])
        blk = 256
        for b in range(tok // blk):
            rows = pl.ds(b * blk, blk)
            width = (b + 1) * blk
            scores = jnp.dot(qf[h, rows, :], kft[h, :, pl.ds(0, width)], preferred_element_type=F32)
            weights = scores.astype(BF16) * mask[rows, pl.ds(0, width)]
            values = jnp.concatenate([vraw[h, pl.ds(0, width), :], ones_v[:width]], axis=1)
            nd[h, rows, :] = jnp.dot(weights, values, preferred_element_type=F32)

    sqacc[...] = jnp.zeros_like(sqacc)

    def finish(p, u):
        h = head_of(p, u)
        carried = car[p, u]
        norm = jnp.broadcast_to(carried[128:129, :], (128, 128)).T
        both = jnp.concatenate([carried[:128, :], norm], axis=1)
        high = both.astype(BF16)
        low = (both - high.astype(F32)).astype(BF16)
        right = jnp.concatenate([high, low], axis=0)

        for b in range(tok // 256):
            rows = pl.ds(b * 256, 256)
            q = qf[h, rows, :] * cmask[rows, :]
            extra = jnp.dot(jnp.concatenate([q, q], axis=1), right, preferred_element_type=F32)
            total = nd[h, rows, :] + extra
            result = total[:, :128] / total[:, 128:]
            att[h, rows, :] = result
            sqacc[rows, :] += result * result

    def late(u):
        @pl.when(z == 0)
        def _():
            handle_5(u, True)

    last_3(0)
    finish(3, 0)
    late(0)
    last_3(1)
    finish(3, 1)
    late(1)
    finish(0, 0)
    finish(0, 1)
    last_2(0)
    finish(2, 0)
    last_1(0)
    finish(1, 0)
    last_2(1)
    finish(2, 1)
    last_1(1)
    finish(1, 1)

    for g in range(groups):
        sq[0, pl.ds(g, 1), :] = jnp.sum(sqacc[pl.ds(g * 128, 128), :].T, axis=0, keepdims=True)

    def send_sq(j):
        return send(sq.at[0], sq.at[j], sq_s.at[j - 1], sq_r.at[j - 1], peer(j))

    for j in range(1, n_head):
        send_sq(j).start()
    @pl.when(wrapped)
    def _():
        for u in range(heads // 4):
            for c in splits:
                for stage in (0, 1):
                    for kind in (0,):
                        send_relay(stage, kind, u, c, xo.at[0, u]).wait_send()

    for u in range(heads // 4):
        for c in splits:
            for p in (1, 2, 3):
                send_w(p, u, c, wo.at[0, u]).wait_send()
            for p in (0, 1, 2):
                send_s(p, u, c, so.at[0, u]).wait_send()
            for kind in (0, 1, 2, 4, 5):
                send_x(kind, u, c, xo.at[0, u]).wait_send()

            @pl.when(z != 0)
            def _():
                send_x(3, u, c, xo.at[0, u]).wait_send()
                send_x(6, u, c, xo.at[0, u]).wait_send()

            @pl.when(z == n_z - 1)
            def _():
                send_x(7, u, c, xo.at[0, u]).wait_send()

    for j in range(1, n_head):
        send_sq(j).wait_recv()
    total = jnp.sum(sq[...], axis=0)
    scale = lax.rsqrt(total / n_feat + 1e-06)
    gains.wait()

    for g in range(groups):
        rows = pl.ds(g * 128, 128)
        factor = jnp.broadcast_to(scale[g : g + 1, :], (128, 128)).T
        for h in range(heads):
            cols = pl.ds(h * E, E)
            weight = gain[cols].astype(F32)[None, :]
            out[rows, cols] = (att[h, rows, :] * factor * weight).astype(BF16)

    for j in range(1, n_head):
        send_sq(j).wait_send()


def body(n_seq, n_head, query_act, key_act, value_act, norm_gain, doc_lengths):
    tok, width = query_act.shape
    heads = width // E
    two = heads // 4
    any_spec = pl.BlockSpec(memory_space=pl.ANY)
    dma = pltpu.SemaphoreType.DMA
    state = lambda n: pltpu.VMEM((n, two, ROWS, 128), F32)
    arrivals = lambda n: dma((n, two, len(PARTS)))
    return pl.pallas_call(
        functools.partial(kernel, n_seq, n_head, n_head * width),
        out_shape=pltpu.VMEM((tok, width), BF16),
        in_specs=[any_spec] * 5,
        out_specs=pl.BlockSpec(memory_space=pltpu.VMEM),
        scratch_shapes=[
            pltpu.VMEM((heads, tok, E), BF16),
            pltpu.VMEM((heads, tok, E), BF16),
            pltpu.VMEM((heads, tok, E), BF16),
            pltpu.VMEM((heads, tok, E), BF16),
            pltpu.VMEM((heads, E, tok), BF16),
            pltpu.VMEM((heads, ROWS, 128), F32),
            pltpu.VMEM((heads, tok, 256), F32),
            pltpu.VMEM((heads, tok, E), F32),
            pltpu.VMEM((tok, 128), F32),
            pltpu.VMEM((tok, tok), BF16),
            pltpu.VMEM((tok, 128), BF16),
            pltpu.VMEM((128, tok), BF16),
            pltpu.VMEM((16, 128), jnp.int32),
            pltpu.VMEM((8, 128), jnp.int32),
            pltpu.SMEM(doc_lengths.shape, jnp.int32),
            pltpu.VMEM((width,), BF16),
            state(3), state(3), state(8),
            state(3), state(3), state(2), state(4),
            pltpu.VMEM((n_head, 8, 128), F32),
            dma((3, heads)), dma((2,)),
            pltpu.VMEM((2, 2, two, ROWS, 128), F32),
            dma((2, 2, two, len(PARTS))), dma((2, 2, two, len(PARTS))),
            arrivals(3), arrivals(3), arrivals(3), arrivals(3),
            arrivals(8), arrivals(8),
            dma((n_head - 1,)), dma((n_head - 1,)),
        ],
        compiler_params=pltpu.CompilerParams(
            collective_id=1, has_side_effects=True, vmem_limit_bytes=56 * 1024 * 1024
        ),
        name="attend",
    )(query_act, key_act, value_act, norm_gain, doc_lengths)


def solution(mesh):
    in_specs = (P("seq", "head"), P("seq", "head"), P("seq", "head"), P("head"), P())
    fn = functools.partial(body, mesh.shape["seq"], mesh.shape["head"])
    return jax.shard_map(fn, mesh=mesh, in_specs=in_specs, out_specs=P("seq", "head"), check_vma=False)
```
